32 devices in a mesh: groups: 2 (over x), orb: 16 (over z, y, core).
Axes of the slice: x: 2, y: 2, z: 4, core: 2. Of those that a mesh axis runs over, the one named last changes fastest.
Arguments:
- pair_list: int32 [2048, 2], P(('groups', 'orb')), parts along dimension 0, may hold values from 0 to 511, as said below
- orbital_slot: int32 [1024], P('groups'), parts along dimension 0, may hold values from 0 to 511, as said below
- blocks: bfloat16 [1024, 512, 128], P(('groups', 'orb')), parts along dimension 0, may hold values from -0.59765625 to 0.59765625
- transforms: bfloat16 [1024, 128, 128], P(('groups', 'orb')), parts along dimension 0, may hold values from -0.5 to 0.5
- domain: int32 [1024, 128], P(('groups', 'orb')), parts along dimension 0, may hold values from 0 to 2047
- eps_virt: float32 [4096], P('groups'), parts along dimension 0, may hold values from 0.2 to 2.5
- eps_occ: float32 [1024], P('groups'), parts along dimension 0, may hold values from -1.5 to -0.3
- offsets: int32 [1024], P('groups'), parts along dimension 0, may hold values from 0 to 3
Outputs:
- pair_energy: float32 [2048], P(('groups', 'orb')), parts along dimension 0
- density: float32 [1024, 128, 128], P(('groups', 'orb')), parts along dimension 0
The draws below stay inside these ranges and needn't reach their ends.
There are 2 independent parts, one for each index of `groups`. The reference program is written for one: setup_inputs(seed, part) draws one part's arguments, and reference() takes and returns one part's arrays. A program takes and returns all parts, laid end to end along the dimension named above; each array names one. Nothing has to cross between parts.
Inputs may be any that keep to these rules, and one draw needn't show every extreme that they name: `pair_list`: the 64 pairs of each aligned block (one device's pairs) have their first orbital stored in that block's device, slots 32 * d to 32 * (d + 1) - 1 for block d. Within one block, the pairs whose second orbital is stored on one device are at most 4, and they all name the same second orbital; this most is reached. No pair names one orbital twice. `orbital_slot`: A permutation of the orbital ids.
All inputs are finite; a program needn't handle non-finite values.
Results may differ from the reference program's by a relative error of at most 0.0022.
Values may be sent and summed in bfloat16 or wider, within the bound.
No kernel may reach another device: no remote copies, remote signals or barrier semaphores. Data moves between devices by JAX's collectives and lax.ppermute only.
A program may use at most 128 MiB of HBM per device.

```python
import jax
import jax.numpy as jnp
from jax import lax

NV = 128
NFIT = 512
AUXBLK = 128
ORB_DEV = 32
PAIR_DEV = 64
ORBS = 512
PAIRS = 1024
NVIRT = 2048
N_ORB = 16


def shuffle_owners(sub_key):
    return jax.random.permutation(sub_key, N_ORB).astype(jnp.int32)


def shuffle_pairs(sub_key):
    return jax.random.permutation(sub_key, PAIR_DEV).astype(jnp.int32)


def pair_layout(key):
    key_list = jax.random.split(key, 6)
    ids_of_slot = jax.random.permutation(key_list[0], ORBS).astype(jnp.int32)
    slot_table = jnp.zeros((ORBS,), jnp.int32).at[ids_of_slot].set(jnp.arange(ORBS, dtype=jnp.int32))
    rounds = (PAIR_DEV + N_ORB - 1) // N_ORB
    owner_rows = jax.vmap(shuffle_owners)(jax.random.split(key_list[1], N_ORB * rounds))
    owner_rows = owner_rows.reshape(N_ORB, rounds * N_ORB)[:, :PAIR_DEV]
    chosen = jax.random.randint(key_list[2], (N_ORB, N_ORB), 0, ORB_DEV).astype(jnp.int32)
    second_local = jnp.take_along_axis(chosen, owner_rows, axis=1)
    first_local = jnp.minimum(jax.random.randint(key_list[3], (N_ORB, PAIR_DEV), 0, ORB_DEV), jax.random.randint(key_list[4], (N_ORB, PAIR_DEV), 0, ORB_DEV)).astype(jnp.int32)
    device_row = jnp.arange(N_ORB, dtype=jnp.int32)[:, None]
    clashing = (owner_rows == device_row) & (first_local == second_local)
    first_local = jnp.where(clashing, (first_local + 1) % ORB_DEV, first_local)
    placing = jax.vmap(shuffle_pairs)(jax.random.split(key_list[5], N_ORB))
    first_slot = jnp.take_along_axis(device_row * ORB_DEV + first_local, placing, axis=1)
    second_slot = jnp.take_along_axis(owner_rows * ORB_DEV + second_local, placing, axis=1)
    pair_table = jnp.stack([ids_of_slot[first_slot], ids_of_slot[second_slot]], axis=-1).reshape(PAIRS, 2)
    return (pair_table.astype(jnp.int32), slot_table)


def draw_pair_list(key, part):
    pair_table, slot_table = pair_layout(key)
    return pair_table


def draw_orbital_slot(key, part):
    pair_table, slot_table = pair_layout(key)
    return slot_table


def set_ends(entries, own_key, least, high):
    shape = entries.shape
    place = [jax.random.randint(jax.random.fold_in(own_key, axis), (), 0, shape[axis]) for axis in range(len(shape))]
    entries = entries.at[tuple(place)].set(least)
    longest = shape.index(max(shape))
    place[longest] = (place[longest] + 1) % shape[longest]
    return entries.at[tuple(place)].set(high)


def levels(key, extent, pieces, smallest, high):
    gain, own = 1.0, jax.random.fold_in(key, 6)
    for dim, parts in pieces:
        steps = jnp.exp(jax.random.uniform(jax.random.fold_in(own, dim), (parts,), jnp.float32, smallest / len(pieces), high / len(pieces)))
        gain = gain * jnp.repeat(steps, extent[dim] // parts).reshape([-1 if axis == dim else 1 for axis in range(len(extent))])
    return gain


def centred(key, shape, spread, bound, shards=(), kind=jnp.bfloat16):
    result = jax.random.normal(key, shape, jnp.float32) * spread
    if len(shards) > 0:
        result = levels(key, shape, shards, -0.22, 0.18) * result
    return jnp.clip(result, min=-bound, max=bound).astype(kind)


def setup_inputs(seed: int = 0, part: int = 0) -> dict:
    splits = jax.random.split(jax.random.key(seed), 9)
    part_splits = jax.random.split(jax.random.fold_in(splits[8], part), 9)
    pair_list = draw_pair_list(jax.random.fold_in(jax.random.fold_in(splits[8], part), 71), part)
    orbital_slot = draw_orbital_slot(jax.random.fold_in(jax.random.fold_in(splits[8], part), 71), part)
    blocks = centred(part_splits[2], (ORBS, NFIT, NV), 0.1, 0.59765625, ((0, 16),))
    transforms = centred(part_splits[3], (ORBS, NV, NV), NV ** -0.5, 0.5, ((0, 16),))
    domain = set_ends(jax.random.randint(part_splits[4], (ORBS, NV), 0, NVIRT), jax.random.fold_in(part_splits[4], 1), 0, NVIRT - 1).astype(jnp.int32)
    eps_virt = jnp.clip(jax.random.uniform(part_splits[5], (NVIRT,), jnp.float32, 0.2, 2.5), 0.2, 2.5)
    eps_occ = jnp.clip(jax.random.uniform(part_splits[6], (ORBS,), jnp.float32, -1.5, -0.3), -1.5, -0.3)
    offsets = set_ends(jax.random.randint(part_splits[7], (ORBS,), 0, 4), jax.random.fold_in(part_splits[7], 1), 0, 3).astype(jnp.int32)
    return dict(pair_list=pair_list, orbital_slot=orbital_slot, blocks=blocks, transforms=transforms, domain=domain, eps_virt=eps_virt, eps_occ=eps_occ, offsets=offsets)


full_precision = lax.Precision.HIGHEST


def align_rows(rows, shift_rows):
    fit_rows = rows.shape[0]
    padded = jnp.pad(rows, ((fit_rows, fit_rows), (0, 0)))
    return lax.dynamic_slice_in_dim(padded, (fit_rows + shift_rows).astype(jnp.int32), fit_rows, 0)


def reference(pair_list, orbital_slot, blocks, transforms, domain, eps_virt, eps_occ, offsets):
    first_slot = orbital_slot[pair_list[:, 0]].astype(jnp.int32)
    second_slot = orbital_slot[pair_list[:, 1]].astype(jnp.int32)
    dom_energy = lax.optimization_barrier(eps_virt[domain].astype(jnp.bfloat16)).astype(jnp.float32)
    rotated = jnp.einsum("srv,svw->srw", blocks.astype(jnp.float32), transforms.astype(jnp.float32), precision=full_precision)
    rotated = lax.optimization_barrier(rotated.astype(jnp.bfloat16)).astype(jnp.float32)
    group_count = PAIRS // PAIR_DEV
    grouped = (first_slot.reshape(group_count, PAIR_DEV), second_slot.reshape(group_count, PAIR_DEV))

    def one_group(inner_sum, slot_pair):
        first_rows, second_rows = slot_pair
        own_rows = rotated[first_rows]
        row_shift = (AUXBLK * (offsets[first_rows] - offsets[second_rows])).astype(jnp.int32)
        aligned = jax.vmap(align_rows)(rotated[second_rows], row_shift)
        coupling = jnp.einsum("prv,prw->pvw", own_rows, aligned, precision=full_precision)
        denominator = dom_energy[first_rows][:, :, None] + dom_energy[second_rows][:, None, :] - (eps_occ[first_rows] + eps_occ[second_rows])[:, None, None]
        amplitude = coupling / denominator
        energy_part = -jnp.sum(coupling * amplitude, axis=(1, 2)) / NV
        amp_half = lax.optimization_barrier(amplitude.astype(jnp.bfloat16)).astype(jnp.float32)
        left_density = jnp.einsum("pab,pcb->pac", amp_half, amp_half, precision=full_precision)
        right_density = jnp.einsum("pab,pac->pbc", amp_half, amp_half, precision=full_precision)
        inner_sum = inner_sum.at[first_rows].add(left_density).at[second_rows].add(right_density)
        return inner_sum, energy_part

    start_sum = jnp.zeros((ORBS, NV, NV), jnp.float32)
    inner_sum, energy_parts = lax.scan(one_group, start_sum, grouped)
    turned = transforms.astype(jnp.float32)
    density = jnp.einsum("sab,sbc->sac", turned, inner_sum, precision=full_precision)
    density = jnp.einsum("sac,sdc->sad", density, turned, precision=full_precision)
    return energy_parts.reshape(PAIRS), density
```

```python
import functools

import jax
import jax.numpy as jnp
from jax import lax
from jax.experimental import pallas as pl
from jax.experimental.pallas import tpu as pltpu
from jax.sharding import PartitionSpec as P

AUXBLK = 128
ENERGY_ROWS = 16
VMEM_LIMIT = 48 * 1024 * 1024

SMEM = functools.partial(pl.BlockSpec, memory_space=pltpu.SMEM)
VMEM = functools.partial(pl.BlockSpec, memory_space=pltpu.VMEM)


def f32_dot(lhs, rhs, dims):
    return lax.dot_general(lhs, rhs, (dims, ((), ())), preferred_element_type=jnp.float32)


def split_dot(lhs, rhs, dims, wide):
    value = (lhs, rhs)[wide]
    high = value.astype(jnp.bfloat16)
    low = (value - high.astype(jnp.float32)).astype(jnp.bfloat16)
    if wide == 0:
        return f32_dot(high, rhs, dims) + f32_dot(low, rhs, dims)
    return f32_dot(lhs, high, dims) + f32_dot(lhs, low, dims)


def plan_kernel(orb_dev, cap, pairs, slots, offsets, eps_occ, wanted, index, first, shift, occupied, seen):
    owners = wanted.shape[0]

    def clear(owner, carry):
        seen[owner] = 0
        return carry

    lax.fori_loop(0, owners, clear, 0)

    def one_pair(pair, carry):
        slot_i = slots[pairs[0, pair]]
        slot_j = slots[pairs[1, pair]]
        owner = lax.div(slot_j, jnp.int32(orb_dev))
        local_j = lax.rem(slot_j, jnp.int32(orb_dev))
        rank = seen[owner]
        seen[owner] = rank + 1
        place = owner * cap + rank
        index[place] = pair
        first[place] = lax.rem(slot_i, jnp.int32(orb_dev))
        shift[place] = offsets[slot_i] - offsets[slot_j]
        occupied[place] = eps_occ[slot_i] + eps_occ[slot_j]
        wanted[owner] = jnp.full(wanted.shape[1:], local_j, jnp.int32)
        return carry

    lax.fori_loop(0, pairs.shape[1], one_pair, 0)


def plan(owners, orb_dev, pair_list, orbital_slot, offsets, eps_occ):
    pair_dev = pair_list.shape[0]
    cap = pair_dev // owners
    sorted_ints = jax.ShapeDtypeStruct((pair_dev,), jnp.int32)
    return pl.pallas_call(
        functools.partial(plan_kernel, orb_dev, cap),
        out_shape=(
            jax.ShapeDtypeStruct((owners, 1, 128), jnp.int32),
            sorted_ints,
            sorted_ints,
            sorted_ints,
            jax.ShapeDtypeStruct((pair_dev,), jnp.float32),
        ),
        in_specs=[SMEM()] * 4,
        out_specs=(VMEM(), SMEM(), SMEM(), SMEM(), SMEM()),
        scratch_shapes=[pltpu.SMEM((owners,), jnp.int32)],
        name="plan",
    )(pair_list.T, orbital_slot, offsets, eps_occ)


def energies_kernel(domain, eps_virt, rows, columns):
    orb_dev, width = domain.shape
    wanted = domain[...]
    line, lane = wanted // 128, wanted % 128
    found = jnp.zeros((orb_dev, width), jnp.float32)
    for k in range(eps_virt.shape[0]):
        spread = jnp.broadcast_to(eps_virt[pl.ds(k, 1), :], (orb_dev, width))
        picked = jnp.take_along_axis(spread, lane, axis=1)
        found = jnp.where(line == k, picked, found)
    found = found.astype(jnp.bfloat16).astype(jnp.float32)
    for s in range(orb_dev):
        row = found[s : s + 1, :]
        rows[s] = row
        columns[s] = jnp.broadcast_to(row, (width, width)).T.astype(jnp.bfloat16)


def domain_energies(domain, eps_virt):
    orb_dev, width = domain.shape
    return pl.pallas_call(
        energies_kernel,
        out_shape=(
            jax.ShapeDtypeStruct((orb_dev, 1, width), jnp.float32),
            jax.ShapeDtypeStruct((orb_dev, width, width), jnp.bfloat16),
        ),
        in_specs=[VMEM()] * 2,
        out_specs=(VMEM(), VMEM()),
        compiler_params=pltpu.CompilerParams(vmem_limit_bytes=VMEM_LIMIT),
        name="domain_energies",
    )(domain, eps_virt.reshape(-1, 128))


def own_kernel(blocks, transforms, turned):
    for s in range(blocks.shape[0]):
        turned[s] = f32_dot(transforms[s], blocks[s], ((0,), (1,))).astype(jnp.bfloat16)


def own_rotated(blocks, transforms, per_step=4):
    orb_dev, fit_rows, width = blocks.shape
    return pl.pallas_call(
        own_kernel,
        grid=(orb_dev // per_step,),
        out_shape=jax.ShapeDtypeStruct((orb_dev, width, fit_rows), jnp.bfloat16),
        in_specs=[
            pl.BlockSpec((per_step, fit_rows, width), lambda g: (g, 0, 0)),
            pl.BlockSpec((per_step, width, width), lambda g: (g, 0, 0)),
        ],
        out_specs=pl.BlockSpec((per_step, width, fit_rows), lambda g: (g, 0, 0)),
        compiler_params=pltpu.CompilerParams(vmem_limit_bytes=VMEM_LIMIT),
        name="own_rotated",
    )(blocks, transforms)


def pack_kernel(per_step, asked, rows, *refs):
    blocks, transforms, message = refs[:per_step], refs[per_step : 2 * per_step], refs[-1]
    fit_rows = blocks[0].shape[1]
    step = pl.program_id(0)
    for k in range(per_step):
        rotated = f32_dot(blocks[k][0], transforms[k][0], ((1,), (0,)))
        message[k, :fit_rows, :] = rotated.astype(jnp.bfloat16)
        energy = rows[asked[step * per_step + k]]
        message[k, fit_rows:, :] = jnp.broadcast_to(energy, (ENERGY_ROWS, energy.shape[1])).astype(
            jnp.bfloat16
        )


def pack_messages(asked, rows, blocks, transforms, per_step=4):
    owners = asked.shape[0]
    orb_dev, fit_rows, width = blocks.shape

    def of_slot(k):
        return lambda g, asked: (asked[g * per_step + k], 0, 0)

    return pl.pallas_call(
        functools.partial(pack_kernel, per_step),
        grid_spec=pltpu.PrefetchScalarGridSpec(
            num_scalar_prefetch=1,
            grid=(owners // per_step,),
            in_specs=[pl.BlockSpec((orb_dev, 1, width), lambda g, asked: (0, 0, 0))]
            + [pl.BlockSpec((1, fit_rows, width), of_slot(k)) for k in range(per_step)]
            + [pl.BlockSpec((1, width, width), of_slot(k)) for k in range(per_step)],
            out_specs=pl.BlockSpec(
                (per_step, fit_rows + ENERGY_ROWS, width), lambda g, asked: (g, 0, 0)
            ),
        ),
        out_shape=jax.ShapeDtypeStruct((owners, fit_rows + ENERGY_ROWS, width), jnp.bfloat16),
        compiler_params=pltpu.CompilerParams(vmem_limit_bytes=VMEM_LIMIT),
        name="pack_messages",
    )(asked, rows, *([blocks] * per_step), *([transforms] * per_step))


def pairs_kernel(cap, first, shift, occupied, message, *refs):
    turned, columns = refs[:cap], refs[cap : 2 * cap]
    half, energy, right, padded = refs[2 * cap :]
    width, fit_rows = turned[0].shape[1:]
    margin = fit_rows - AUXBLK
    step = pl.program_id(0)

    @pl.when(step == 0)
    def _():
        zeros = jnp.zeros((margin, width), jnp.bfloat16)
        padded[:margin, :] = zeros
        padded[margin + fit_rows :, :] = zeros

    padded[margin : margin + fit_rows, :] = message[0, :fit_rows, :]
    far = message[0, fit_rows:, :].astype(jnp.float32)[:1, :]
    for k in range(cap):
        place = step * cap + k
        begin = pl.multiple_of(margin + AUXBLK * shift[place], AUXBLK)
        aligned = padded[pl.ds(begin, fit_rows), :]
        coupling = f32_dot(turned[k][0], aligned, ((1,), (0,)))
        denominator = (columns[k][0].astype(jnp.float32) + far) - occupied[place]
        amplitude = coupling / denominator
        energy[k] = jnp.sum(coupling * amplitude, axis=0, keepdims=True)
        half[k] = amplitude.astype(jnp.bfloat16)
    stacked = half[...].reshape(cap * width, width)
    right[0] = f32_dot(stacked, stacked, ((0,), (0,))).astype(jnp.bfloat16)


def pair_terms(first, shift, occupied, messages, turned, columns):
    owners, rows, width = messages.shape
    pair_dev = first.shape[0]
    cap = pair_dev // owners
    fit_rows = turned.shape[2]

    def of_pair(k):
        return lambda g, first, shift, occupied: (first[g * cap + k], 0, 0)

    def of_step(g, first, shift, occupied):
        return (g, 0, 0)

    return pl.pallas_call(
        functools.partial(pairs_kernel, cap),
        grid_spec=pltpu.PrefetchScalarGridSpec(
            num_scalar_prefetch=3,
            grid=(owners,),
            in_specs=[pl.BlockSpec((1, rows, width), of_step)]
            + [pl.BlockSpec((1, width, fit_rows), of_pair(k)) for k in range(cap)]
            + [pl.BlockSpec((1, width, width), of_pair(k)) for k in range(cap)],
            out_specs=(
                pl.BlockSpec((cap, width, width), of_step),
                pl.BlockSpec((cap, 1, width), of_step),
                pl.BlockSpec((1, width, width), of_step),
            ),
            scratch_shapes=[pltpu.VMEM((3 * fit_rows - 2 * AUXBLK, width), jnp.bfloat16)],
        ),
        out_shape=(
            jax.ShapeDtypeStruct((pair_dev, width, width), jnp.bfloat16),
            jax.ShapeDtypeStruct((pair_dev, 1, width), jnp.float32),
            jax.ShapeDtypeStruct((owners, width, width), jnp.bfloat16),
        ),
        compiler_params=pltpu.CompilerParams(vmem_limit_bytes=VMEM_LIMIT),
        name="pair_terms",
    )(first, shift, occupied, messages, *([turned] * cap), *([columns] * cap))


def left_kernel(index, first, half, energy, inner, pair_energy, scattered):
    width = half.shape[2]
    inner[...] = jnp.zeros_like(inner)

    def one_pair(place, carry):
        amplitude = half[place]
        slot = first[place]
        inner[slot] = inner[slot] + f32_dot(amplitude, amplitude, ((1,), (1,)))
        scattered[index[place]] = energy[place]
        return carry

    lax.fori_loop(0, half.shape[0], one_pair, 0, unroll=4)
    gathered = scattered[...].reshape(half.shape[0], width)
    pair_energy[...] = -jnp.sum(gathered, axis=1, keepdims=True) / width


def left_sums(orb_dev, index, first, half, energy):
    pair_dev, width, _ = half.shape
    return pl.pallas_call(
        left_kernel,
        in_specs=[SMEM(), SMEM(), VMEM(), VMEM()],
        out_specs=(VMEM(), VMEM()),
        out_shape=(
            jax.ShapeDtypeStruct((orb_dev, width, width), jnp.float32),
            jax.ShapeDtypeStruct((pair_dev, 1), jnp.float32),
        ),
        scratch_shapes=[pltpu.VMEM((pair_dev, 1, width), jnp.float32)],
        compiler_params=pltpu.CompilerParams(vmem_limit_bytes=VMEM_LIMIT),
        name="left_sums",
    )(index, first, half, energy)


def density_kernel(asked, inner, right, transforms, density):
    orb_dev = inner.shape[0]
    density[...] = inner[...]

    def one_message(device, carry):
        slot = asked[device]
        density[slot] = density[slot] + right[device].astype(jnp.float32)
        return carry

    lax.fori_loop(0, right.shape[0], one_message, 0)

    def one_slot(slot, carry):
        turn = transforms[slot]
        half_way = split_dot(turn, density[slot], ((1,), (0,)), 1)
        density[slot] = split_dot(half_way, turn, ((1,), (1,)), 0)
        return carry

    lax.fori_loop(0, orb_dev, one_slot, 0, unroll=4)


def final_density(asked, inner, right, transforms):
    return pl.pallas_call(
        density_kernel,
        in_specs=[SMEM(), VMEM(), VMEM(), VMEM()],
        out_specs=VMEM(),
        out_shape=jax.ShapeDtypeStruct(inner.shape, jnp.float32),
        compiler_params=pltpu.CompilerParams(vmem_limit_bytes=VMEM_LIMIT),
        name="final_density",
    )(asked, inner, right, transforms)


def exchange(messages):
    return lax.all_to_all(messages, "orb", split_axis=0, concat_axis=0, tiled=True)


def local(pair_list, orbital_slot, blocks, transforms, domain, eps_virt, eps_occ, offsets):
    owners = lax.axis_size("orb")
    orb_dev = blocks.shape[0]
    wanted, index, first, shift, occupied = plan(
        owners, orb_dev, pair_list, orbital_slot, offsets, eps_occ
    )
    asked = exchange(wanted)[:, 0, 0]
    rows, columns = domain_energies(domain, eps_virt)
    turned = own_rotated(blocks, transforms)
    incoming = exchange(pack_messages(asked, rows, blocks, transforms))
    half, energy, right = pair_terms(first, shift, occupied, incoming, turned, columns)
    came_back = exchange(right)
    inner, pair_energy = left_sums(orb_dev, index, first, half, energy)
    density = final_density(asked, inner, came_back, transforms)
    return (pair_energy.reshape(-1), density)


def solution(mesh):
    in_specs = (
        P(("groups", "orb"), None),
        P("groups"),
        P(("groups", "orb"), None, None),
        P(("groups", "orb"), None, None),
        P(("groups", "orb"), None),
        P("groups"),
        P("groups"),
        P("groups"),
    )
    out_specs = (P(("groups", "orb")), P(("groups", "orb"), None, None))
    return jax.shard_map(local, mesh=mesh, in_specs=in_specs, out_specs=out_specs, check_vma=False)
```

```python
import functools

import jax
import jax.numpy as jnp
from jax import lax
from jax.experimental import pallas as pl
from jax.experimental.pallas import tpu as pltpu
from jax.sharding import PartitionSpec as P

AUXBLK = 128
ENERGY_ROWS = 16
DIAGONAL_ROWS = 16
MIB = 1024 * 1024

SMEM = functools.partial(pl.BlockSpec, memory_space=pltpu.SMEM)
VMEM = functools.partial(pl.BlockSpec, memory_space=pltpu.VMEM)
ANY = functools.partial(pl.BlockSpec, memory_space=pl.ANY)


def in_hbm(array):
    return pltpu.with_memory_space_constraint(array, pltpu.HBM)


def f32_dot(lhs, rhs, dims):
    return lax.dot_general(lhs, rhs, (dims, ((), ())), preferred_element_type=jnp.float32)


def in_two_parts(value):
    high = value.astype(jnp.bfloat16)
    return high, (value - high.astype(jnp.float32)).astype(jnp.bfloat16)


def turned(turn, inner):
    width = inner.shape[1]
    both = f32_dot(turn, jnp.concatenate(in_two_parts(inner), axis=1), ((1,), (0,)))
    return both[:, :width] + both[:, width:]


def turned_back(half_way, turn):
    height = half_way.shape[0]
    both = f32_dot(jnp.concatenate(in_two_parts(half_way), axis=0), turn, ((1,), (1,)))
    return both[:height] + both[height:]


def plan_kernel(orb_dev, cap, pairs, slots, offsets, eps_occ, wanted, index, first, shift, occupied, seen):
    owners = wanted.shape[0]

    def clear(owner, carry):
        seen[owner] = 0
        return carry

    lax.fori_loop(0, owners, clear, 0, unroll=8)

    def one_pair(pair, carry):
        slot_i = slots[pairs[0, pair]]
        slot_j = slots[pairs[1, pair]]
        owner = lax.div(slot_j, jnp.int32(orb_dev))
        local_j = lax.rem(slot_j, jnp.int32(orb_dev))
        rank = seen[owner]
        seen[owner] = rank + 1
        place = owner * cap + rank
        index[place] = pair
        first[place] = lax.rem(slot_i, jnp.int32(orb_dev))
        shift[place] = offsets[slot_i] - offsets[slot_j]
        occupied[place] = eps_occ[slot_i] + eps_occ[slot_j]
        wanted[owner] = jnp.full(wanted.shape[1:], local_j, jnp.int32)
        return carry

    lax.fori_loop(0, pairs.shape[1], one_pair, 0, unroll=8)


def plan(owners, orb_dev, pair_list, orbital_slot, offsets, eps_occ):
    pair_dev = pair_list.shape[0]
    cap = pair_dev // owners
    sorted_ints = pltpu.HBM((pair_dev,), jnp.int32)
    return pl.pallas_call(
        functools.partial(plan_kernel, orb_dev, cap),
        out_shape=(
            pltpu.HBM((owners, 1, 128), jnp.int32),
            sorted_ints,
            sorted_ints,
            sorted_ints,
            pltpu.HBM((pair_dev,), jnp.float32),
        ),
        in_specs=[SMEM()] * 4,
        out_specs=(VMEM(), SMEM(), SMEM(), SMEM(), SMEM()),
        scratch_shapes=[pltpu.SMEM((owners,), jnp.int32)],
        name="plan",
    )(*map(in_hbm, (pair_list.T, orbital_slot, offsets, eps_occ)))


def energies_kernel(domain, eps_virt, rows):
    orb_dev, width = domain.shape
    wanted = domain[...]
    line, lane = wanted // 128, wanted % 128
    found = jnp.zeros((orb_dev, width), jnp.float32)
    for k in range(eps_virt.shape[0]):
        spread = jnp.broadcast_to(eps_virt[pl.ds(k, 1), :], (orb_dev, width))
        picked = jnp.take_along_axis(spread, lane, axis=1)
        found = jnp.where(line == k, picked, found)
    found = found.astype(jnp.bfloat16).astype(jnp.float32)
    for s in range(orb_dev):
        rows[s] = found[s : s + 1, :]


def domain_energies(domain, eps_virt):
    orb_dev, width = domain.shape
    return pl.pallas_call(
        energies_kernel,
        in_specs=[VMEM()] * 2,
        out_specs=VMEM(),
        out_shape=pltpu.HBM((orb_dev, 1, width), jnp.float32),
        name="domain_energies",
    )(*map(in_hbm, (domain, eps_virt.reshape(-1, 128))))


def own_kernel(chunk, blocks, transforms, held, block_rows, turns, made, arrived, left):
    chunks = blocks.shape[0] // chunk

    def coming(c):
        part = pl.ds(c * chunk, chunk)
        return (
            pltpu.make_async_copy(blocks.at[part], block_rows.at[part], arrived.at[0, c]),
            pltpu.make_async_copy(transforms.at[part], turns.at[part], arrived.at[1, c]),
        )

    def going(c):
        part = pl.ds(c * chunk, chunk)
        return pltpu.make_async_copy(made.at[part], held.at[part], left.at[c])

    for c in range(chunks):
        for copy in coming(c):
            copy.start()

    def one_chunk(c, carry):
        for copy in coming(c):
            copy.wait()
        slots = [c * chunk + u for u in range(chunk)]
        rotated = [f32_dot(block_rows[slot], turns[slot], ((1,), (0,))) for slot in slots]
        for slot, one in zip(slots, rotated):
            made[slot] = one.astype(jnp.bfloat16)
        going(c).start()
        return carry

    lax.fori_loop(0, chunks, one_chunk, 0)
    for c in range(chunks):
        going(c).wait()


def own_rotated(blocks, transforms, chunk=4):
    orb_dev = blocks.shape[0]
    return pl.pallas_call(
        functools.partial(own_kernel, chunk),
        in_specs=[ANY()] * 2,
        out_specs=ANY(),
        out_shape=pltpu.HBM(blocks.shape, jnp.bfloat16),
        scratch_shapes=[
            pltpu.VMEM(blocks.shape, jnp.bfloat16),
            pltpu.VMEM(transforms.shape, jnp.bfloat16),
            pltpu.VMEM(blocks.shape, jnp.bfloat16),
            pltpu.SemaphoreType.DMA((2, orb_dev // chunk)),
            pltpu.SemaphoreType.DMA((orb_dev // chunk,)),
        ],
        compiler_params=pltpu.CompilerParams(vmem_limit_bytes=16 * MIB),
        name="own_rotated",
    )(*map(in_hbm, (blocks, transforms)))


def pack_kernel(
    batch, asked, rows, blocks, transforms, messages, block_rows, turns, made, arrived, left
):
    owners = messages.shape[0]
    fit_rows, width = blocks.shape[1:]

    def coming(owner):
        slot = asked[owner, 0, 0]
        return (
            pltpu.make_async_copy(blocks.at[slot], block_rows.at[owner], arrived.at[0, owner]),
            pltpu.make_async_copy(transforms.at[slot], turns.at[owner], arrived.at[1, owner]),
        )

    def going(owner):
        return pltpu.make_async_copy(made.at[owner], messages.at[owner], left.at[owner])

    def start(owner, carry):
        for copy in coming(owner):
            copy.start()
        return carry

    def forward(b, carry):
        group = [b * batch + u for u in range(batch)]
        for owner in group:
            for copy in coming(owner):
                copy.wait()
        rotated = [f32_dot(block_rows[owner], turns[owner], ((1,), (0,))) for owner in group]
        for owner, one in zip(group, rotated):
            made[owner, :fit_rows, :] = one.astype(jnp.bfloat16)
            energy = rows[asked[owner, 0, 0]]
            made[owner, fit_rows:, :] = jnp.broadcast_to(energy, (ENERGY_ROWS, width)).astype(
                jnp.bfloat16
            )
        for owner in group:
            going(owner).start()
        return carry

    def finish(owner, carry):
        going(owner).wait()
        return carry

    lax.fori_loop(0, owners, start, 0)
    lax.fori_loop(0, owners // batch, forward, 0)
    lax.fori_loop(0, owners, finish, 0)


def pack_messages(asked, rows, blocks, transforms, batch=4):
    owners = asked.shape[0]
    _, fit_rows, width = blocks.shape
    shape = (owners, fit_rows + ENERGY_ROWS, width)
    return pl.pallas_call(
        functools.partial(pack_kernel, batch),
        in_specs=[SMEM(), VMEM(), ANY(), ANY()],
        out_specs=ANY(),
        out_shape=pltpu.HBM(shape, jnp.bfloat16),
        scratch_shapes=[
            pltpu.VMEM((owners, fit_rows, width), jnp.bfloat16),
            pltpu.VMEM((owners, width, width), jnp.bfloat16),
            pltpu.VMEM(shape, jnp.bfloat16),
            pltpu.SemaphoreType.DMA((2, owners)),
            pltpu.SemaphoreType.DMA((owners,)),
        ],
        compiler_params=pltpu.CompilerParams(vmem_limit_bytes=(2 + owners // 2) * MIB),
        name="pack_messages",
    )(asked, *map(in_hbm, (rows, blocks, transforms)))


def fold_symmetric(full):
    width = full.shape[0]
    mid = width // 2
    row = lax.broadcasted_iota(jnp.int32, (mid, width), 0)
    lane = lax.broadcasted_iota(jnp.int32, (mid, width), 1)
    upper, lower = full[:mid, :], full[mid:, :]
    folded = jnp.where(lane <= row + mid, pltpu.roll(upper, mid, 1), lower)
    diagonal = jnp.sum(jnp.where(lane == row + mid, lower, 0.0), axis=0, keepdims=True)
    return jnp.concatenate([folded, jnp.broadcast_to(diagonal, (DIAGONAL_ROWS, width))], axis=0)


def unfold_symmetric(folded):
    width = folded.shape[1]
    mid = width // 2
    row = lax.broadcasted_iota(jnp.int32, (mid, width), 0)
    lane = lax.broadcasted_iota(jnp.int32, (mid, width), 1)
    body, diagonal = folded[:mid, :], folded[mid : mid + 1, :]
    moved = pltpu.roll(body, mid, 1)
    upper = jnp.where(lane < row, moved, 0.0) + jnp.where(lane >= mid, moved, 0.0)
    upper = upper + jnp.where(lane == row, 0.5 * moved, 0.0)
    lower = jnp.where(lane > row + mid, body, 0.0)
    lower = lower + jnp.where(lane == row + mid, 0.5 * diagonal, 0.0)
    once = jnp.concatenate([upper, lower], axis=0)
    return once + once.T


def pairs_kernel(
    cap, batch, first, shift, occupied, rows, held, came, half, energy, right, made, left
):
    steps, height, width = came.shape
    fit_rows = height - ENERGY_ROWS
    block_count = fit_rows // AUXBLK

    def going(b):
        part = pl.ds(b * batch * cap, batch * cap)
        return pltpu.make_async_copy(made.at[part], half.at[part], left.at[b])

    def shifted(place):
        moved = []
        for block in range(block_count):
            source = block - shift[place]
            inside = (source >= 0) & (source < block_count)
            begin = pl.multiple_of(jnp.clip(source, 0, block_count - 1) * AUXBLK, AUXBLK)
            part = held[first[place], pl.ds(begin, AUXBLK), :]
            moved.append(jnp.where(inside, part, jnp.zeros_like(part)))
        return jnp.concatenate(moved, axis=0)

    def one_batch(b, carry):
        group = [b * batch + u for u in range(batch)]
        couplings, far = [], []
        for step in group:
            side = jnp.concatenate([shifted(step * cap + k) for k in range(cap)], axis=1)
            couplings.append(f32_dot(came[step, :fit_rows, :].T, side, ((1,), (0,))))
            row = came[step, fit_rows:, :].astype(jnp.float32)[:1, :]
            far.append(jnp.broadcast_to(row, (width, width)).T)
        for u, step in enumerate(group):
            halves = []
            for k in range(cap):
                place = step * cap + k
                coupling = couplings[u][:, k * width : (k + 1) * width]
                amplitude = coupling / (far[u] + (rows[first[place]] - occupied[place]))
                energy[place] = jnp.sum(coupling * amplitude, axis=0, keepdims=True)
                halves.append(amplitude.astype(jnp.bfloat16))
                made[place] = halves[-1]
            side = jnp.concatenate(halves, axis=1)
            density = f32_dot(side, side, ((1,), (1,)))
            right[step] = fold_symmetric(density).astype(jnp.bfloat16)
        going(b).start()
        return carry

    def finish(b, carry):
        going(b).wait()
        return carry

    lax.fori_loop(0, steps // batch, one_batch, 0)
    lax.fori_loop(0, steps // batch, finish, 0)


def pair_terms(first, shift, occupied, rows, held, messages, batch=8):
    steps, height, width = messages.shape
    pair_dev = first.shape[0]
    cap = pair_dev // steps
    return pl.pallas_call(
        functools.partial(pairs_kernel, cap, batch),
        in_specs=[SMEM()] * 3 + [VMEM()] * 3,
        out_specs=(ANY(), VMEM(), VMEM()),
        out_shape=(
            pltpu.HBM((pair_dev, width, width), jnp.bfloat16),
            pltpu.HBM((pair_dev, 1, width), jnp.float32),
            pltpu.HBM((steps, width // 2 + DIAGONAL_ROWS, width), jnp.bfloat16),
        ),
        scratch_shapes=[
            pltpu.VMEM((pair_dev, width, width), jnp.bfloat16),
            pltpu.SemaphoreType.DMA((steps // batch,)),
        ],
        compiler_params=pltpu.CompilerParams(vmem_limit_bytes=24 * MIB),
        name="pair_terms",
    )(*map(in_hbm, (first, shift, occupied, rows)), held, messages)


def left_kernel(
    batch, index, first, half, energy, transforms, density, pair_energy, halves, turns, inner, scattered, arrived
):
    orb_dev, width, _ = inner.shape
    pair_dev = half.shape[0]
    loads = [
        pltpu.make_async_copy(half, halves, arrived.at[0]),
        pltpu.make_async_copy(transforms, turns, arrived.at[1]),
    ]
    for load in loads:
        load.start()
    inner[...] = jnp.zeros_like(inner)
    for load in loads:
        load.wait()

    def some_pairs(b, carry):
        places = [b * batch + u for u in range(batch)]
        sums = [f32_dot(halves[place], halves[place], ((0,), (0,))) for place in places]
        for place, one in zip(places, sums):
            slot = first[place]
            inner[slot] = inner[slot] + one
            scattered[index[place]] = energy[place]
        return carry

    lax.fori_loop(0, pair_dev // batch, some_pairs, 0)

    def some_slots(b, carry):
        slots = [b * batch + u for u in range(batch)]
        half_way = [turned(turns[slot], inner[slot]) for slot in slots]
        for slot, one in zip(slots, half_way):
            density[slot] = turned_back(one, turns[slot])
        return carry

    lax.fori_loop(0, orb_dev // batch, some_slots, 0)
    gathered = scattered[...].reshape(pair_dev, width)
    pair_energy[...] = -jnp.sum(gathered.T, axis=0, keepdims=True) / width


def left_density(index, first, half, energy, transforms, batch=8):
    orb_dev = transforms.shape[0]
    pair_dev, width, _ = half.shape
    return pl.pallas_call(
        functools.partial(left_kernel, batch),
        in_specs=[SMEM(), SMEM(), ANY(), VMEM(), ANY()],
        out_specs=(VMEM(), VMEM()),
        out_shape=(
            pltpu.HBM((orb_dev, width, width), jnp.float32),
            pltpu.HBM((1, pair_dev), jnp.float32),
        ),
        scratch_shapes=[
            pltpu.VMEM(half.shape, jnp.bfloat16),
            pltpu.VMEM(transforms.shape, jnp.bfloat16),
            pltpu.VMEM((orb_dev, width, width), jnp.float32),
            pltpu.VMEM((pair_dev, 1, width), jnp.float32),
            pltpu.SemaphoreType.DMA((2,)),
        ],
        compiler_params=pltpu.CompilerParams(vmem_limit_bytes=16 * MIB),
        name="left_density",
    )(*map(in_hbm, (index, first, half, energy, transforms)))


def right_kernel(
    batch, asked, density, rights, transforms, out, total, turns, arrived, left
):
    loads = [
        pltpu.make_async_copy(transforms, turns, arrived.at[0]),
        pltpu.make_async_copy(density, total, arrived.at[1]),
    ]
    for load in loads:
        load.start()
    for load in loads:
        load.wait()

    def some_messages(b, carry):
        slots = [asked[b * batch + u, 0, 0] for u in range(batch)]
        inner = [
            unfold_symmetric(rights[b * batch + u].astype(jnp.float32)).astype(jnp.bfloat16)
            for u in range(batch)
        ]
        half_way = [f32_dot(turns[slot], one, ((1,), (0,))) for slot, one in zip(slots, inner)]
        parts = [turned_back(one, turns[slot]) for slot, one in zip(slots, half_way)]
        for slot, part in zip(slots, parts):
            total[slot] = total[slot] + part
        return carry

    lax.fori_loop(0, rights.shape[0] // batch, some_messages, 0)
    store = pltpu.make_async_copy(total, out, left.at[0])
    store.start()
    store.wait()


def add_right_density(asked, density, right, transforms, batch=8):
    return pl.pallas_call(
        functools.partial(right_kernel, batch),
        in_specs=[SMEM(), ANY(), VMEM(), ANY()],
        out_specs=ANY(),
        out_shape=pltpu.HBM(density.shape, jnp.float32),
        scratch_shapes=[
            pltpu.VMEM(density.shape, jnp.float32),
            pltpu.VMEM(transforms.shape, jnp.bfloat16),
            pltpu.SemaphoreType.DMA((2,)),
            pltpu.SemaphoreType.DMA((1,)),
        ],
        compiler_params=pltpu.CompilerParams(vmem_limit_bytes=16 * MIB),
        name="add_right_density",
    )(asked, in_hbm(density), right, in_hbm(transforms))


def exchange(messages):
    return lax.all_to_all(messages, "orb", split_axis=0, concat_axis=0, tiled=True)


def local(pair_list, orbital_slot, blocks, transforms, domain, eps_virt, eps_occ, offsets):
    owners = lax.axis_size("orb")
    orb_dev = blocks.shape[0]
    wanted, index, first, shift, occupied = plan(
        owners, orb_dev, pair_list, orbital_slot, offsets, eps_occ
    )
    asked = exchange(wanted)
    rows = domain_energies(domain, eps_virt)
    incoming = exchange(pack_messages(asked, rows, blocks, transforms))
    held = own_rotated(blocks, transforms)
    half, energy, right = pair_terms(first, shift, occupied, rows, held, incoming)
    came_back = exchange(right)
    density, pair_energy = left_density(index, first, half, energy, transforms)
    density = add_right_density(asked, density, came_back, transforms)
    return (pair_energy.reshape(-1), density)


def solution(mesh):
    in_specs = (
        P(("groups", "orb"), None),
        P("groups"),
        P(("groups", "orb"), None, None),
        P(("groups", "orb"), None, None),
        P(("groups", "orb"), None),
        P("groups"),
        P("groups"),
        P("groups"),
    )
    out_specs = (P(("groups", "orb")), P(("groups", "orb"), None, None))
    return jax.shard_map(local, mesh=mesh, in_specs=in_specs, out_specs=out_specs, check_vma=False)
```

```python
import functools

import jax
import jax.numpy as jnp
from jax import lax
from jax.experimental import pallas as pl
from jax.experimental.pallas import tpu as pltpu
from jax.sharding import PartitionSpec as P

AUXBLK = 128
ENERGY_ROWS = 16
DIAGONAL_ROWS = 16
MIB = 1024 * 1024

SMEM = functools.partial(pl.BlockSpec, memory_space=pltpu.SMEM)
VMEM = functools.partial(pl.BlockSpec, memory_space=pltpu.VMEM)
ANY = functools.partial(pl.BlockSpec, memory_space=pl.ANY)


def in_hbm(array):
    return pltpu.with_memory_space_constraint(array, pltpu.HBM)


def f32_dot(lhs, rhs, dims):
    return lax.dot_general(lhs, rhs, (dims, ((), ())), preferred_element_type=jnp.float32)


def in_two_parts(value):
    high = value.astype(jnp.bfloat16)
    return high, (value - high.astype(jnp.float32)).astype(jnp.bfloat16)


def turned(turn, inner):
    width = inner.shape[1]
    both = f32_dot(turn, jnp.concatenate(in_two_parts(inner), axis=1), ((1,), (0,)))
    return both[:, :width] + both[:, width:]


def turned_back(half_way, turn):
    height = half_way.shape[0]
    both = f32_dot(jnp.concatenate(in_two_parts(half_way), axis=0), turn, ((1,), (1,)))
    return both[:height] + both[height:]


def wanted_kernel(orb_dev, mask, pairs, slots, wanted):
    def one_pair(pair, carry):
        slot = slots[pairs[1, pair]]
        owner = lax.div(slot, jnp.int32(orb_dev))
        local_slot = lax.rem(slot, jnp.int32(orb_dev))
        wanted[owner ^ mask] = jnp.full(wanted.shape[1:], local_slot, jnp.int32)
        return carry

    lax.fori_loop(0, pairs.shape[1], one_pair, 0, unroll=16)


def wanted_slots(owners, orb_dev, mask, pair_list, orbital_slot):
    return pl.pallas_call(
        functools.partial(wanted_kernel, orb_dev, mask),
        out_shape=pltpu.HBM((owners, 1, 128), jnp.int32),
        in_specs=[SMEM()] * 2,
        out_specs=VMEM(),
        name="wanted_slots",
    )(*map(in_hbm, (pair_list.T, orbital_slot)))


def plan_kernel(orb_dev, cap, pairs, slots, offsets, eps_occ, index, first, shift, occupied, seen):
    owners = seen.shape[0]

    def clear(owner, carry):
        seen[owner] = 0
        return carry

    lax.fori_loop(0, owners, clear, 0, unroll=8)

    def one_pair(pair, carry):
        slot_i = slots[pairs[0, pair]]
        slot_j = slots[pairs[1, pair]]
        owner = lax.div(slot_j, jnp.int32(orb_dev))
        rank = seen[owner]
        seen[owner] = rank + 1
        place = owner * cap + rank
        index[place] = pair
        first[place] = lax.rem(slot_i, jnp.int32(orb_dev))
        shift[place] = offsets[slot_i] - offsets[slot_j]
        occupied[place] = eps_occ[slot_i] + eps_occ[slot_j]
        return carry

    lax.fori_loop(0, pairs.shape[1], one_pair, 0, unroll=8)


def plan(owners, orb_dev, pair_list, orbital_slot, offsets, eps_occ):
    pair_dev = pair_list.shape[0]
    cap = pair_dev // owners
    sorted_ints = pltpu.HBM((pair_dev,), jnp.int32)
    return pl.pallas_call(
        functools.partial(plan_kernel, orb_dev, cap),
        out_shape=(
            sorted_ints,
            sorted_ints,
            sorted_ints,
            pltpu.HBM((pair_dev,), jnp.float32),
        ),
        in_specs=[SMEM()] * 4,
        out_specs=(SMEM(), SMEM(), SMEM(), SMEM()),
        scratch_shapes=[pltpu.SMEM((owners,), jnp.int32)],
        name="plan",
    )(*map(in_hbm, (pair_list.T, orbital_slot, offsets, eps_occ)))


def own_kernel(
    chunk, domain, eps_virt, blocks, transforms, rows, held, block_rows, turns, made, arrived, left
):
    orb_dev, fit_rows, width = blocks.shape
    chunks = orb_dev // chunk

    def coming(c):
        part = pl.ds(c * chunk, chunk)
        return (
            pltpu.make_async_copy(blocks.at[part], block_rows.at[part], arrived.at[0, c]),
            pltpu.make_async_copy(transforms.at[part], turns.at[part], arrived.at[1, c]),
        )

    def going(c):
        part = pl.ds(c * chunk, chunk)
        return pltpu.make_async_copy(made.at[part], held.at[part], left.at[c])

    for c in range(chunks):
        for copy in coming(c):
            copy.start()
    wanted = domain[...]
    line, lane = wanted // 128, wanted % 128
    found = jnp.zeros((orb_dev, width), jnp.float32)
    for k in range(eps_virt.shape[0]):
        spread = jnp.broadcast_to(eps_virt[pl.ds(k, 1), :], (orb_dev, width))
        picked = jnp.take_along_axis(spread, lane, axis=1)
        found = jnp.where(line == k, picked, found)
    rounded = found.astype(jnp.bfloat16).astype(jnp.float32)
    for s in range(orb_dev):
        row = rounded[s : s + 1, :]
        rows[s] = row
        made[s, fit_rows:, :] = jnp.broadcast_to(row, (ENERGY_ROWS, width)).astype(jnp.bfloat16)

    def one_chunk(c, carry):
        for copy in coming(c):
            copy.wait()
        slots = [c * chunk + u for u in range(chunk)]
        rotated = [f32_dot(block_rows[slot], turns[slot], ((1,), (0,))) for slot in slots]
        for slot, one in zip(slots, rotated):
            made[slot, :fit_rows, :] = one.astype(jnp.bfloat16)
        going(c).start()
        return carry

    lax.fori_loop(0, chunks, one_chunk, 0)
    for c in range(chunks):
        going(c).wait()


def own_rotated(domain, eps_virt, blocks, transforms, chunk=4):
    orb_dev, fit_rows, width = blocks.shape
    shape = (orb_dev, fit_rows + ENERGY_ROWS, width)
    return pl.pallas_call(
        functools.partial(own_kernel, chunk),
        in_specs=[VMEM(), VMEM(), ANY(), ANY()],
        out_specs=(VMEM(), ANY()),
        out_shape=(
            pltpu.HBM((orb_dev, 1, width), jnp.float32),
            pltpu.HBM(shape, jnp.bfloat16),
        ),
        scratch_shapes=[
            pltpu.VMEM(blocks.shape, jnp.bfloat16),
            pltpu.VMEM(transforms.shape, jnp.bfloat16),
            pltpu.VMEM(shape, jnp.bfloat16),
            pltpu.SemaphoreType.DMA((2, orb_dev // chunk)),
            pltpu.SemaphoreType.DMA((orb_dev // chunk,)),
        ],
        compiler_params=pltpu.CompilerParams(vmem_limit_bytes=16 * MIB),
        name="own_rotated",
    )(*map(in_hbm, (domain, eps_virt.reshape(-1, 128), blocks, transforms)))


def pack_kernel(asked_mask, mask, asked, held, messages, made, arrived, left):
    owners = messages.shape[0]

    def coming(owner):
        source = held.at[asked[owner ^ asked_mask, 0, 0]]
        return pltpu.make_async_copy(source, made.at[owner], arrived.at[owner])

    def going(owner):
        return pltpu.make_async_copy(made.at[owner], messages.at[owner ^ mask], left.at[owner])

    def start(owner, carry):
        coming(owner).start()
        return carry

    def forward(owner, carry):
        coming(owner).wait()
        going(owner).start()
        return carry

    def finish(owner, carry):
        going(owner).wait()
        return carry

    for step in (start, forward, finish):
        lax.fori_loop(0, owners, step, 0, unroll=4)


def pack_messages(asked_mask, mask, asked, held):
    owners = asked.shape[0]
    shape = (owners,) + held.shape[1:]
    return pl.pallas_call(
        functools.partial(pack_kernel, asked_mask, mask),
        in_specs=[SMEM(), ANY()],
        out_specs=ANY(),
        out_shape=pltpu.HBM(shape, jnp.bfloat16),
        scratch_shapes=[
            pltpu.VMEM(shape, jnp.bfloat16),
            pltpu.SemaphoreType.DMA((owners,)),
            pltpu.SemaphoreType.DMA((owners,)),
        ],
        compiler_params=pltpu.CompilerParams(vmem_limit_bytes=16 * MIB),
        name="pack_messages",
    )(asked, in_hbm(held))


def fold_symmetric(full):
    width = full.shape[0]
    mid = width // 2
    row = lax.broadcasted_iota(jnp.int32, (mid, width), 0)
    lane = lax.broadcasted_iota(jnp.int32, (mid, width), 1)
    upper, lower = full[:mid, :], full[mid:, :]
    folded = jnp.where(lane <= row + mid, pltpu.roll(upper, mid, 1), lower)
    diagonal = jnp.sum(jnp.where(lane == row + mid, lower, 0.0), axis=0, keepdims=True)
    return jnp.concatenate([folded, jnp.broadcast_to(diagonal, (DIAGONAL_ROWS, width))], axis=0)


def unfold_symmetric(folded):
    width = folded.shape[1]
    mid = width // 2
    row = lax.broadcasted_iota(jnp.int32, (mid, width), 0)
    lane = lax.broadcasted_iota(jnp.int32, (mid, width), 1)
    body, diagonal = folded[:mid, :], folded[mid : mid + 1, :]
    moved = pltpu.roll(body, mid, 1)
    upper = jnp.where(lane < row, moved, 0.0) + jnp.where(lane >= mid, moved, 0.0)
    upper = upper + jnp.where(lane == row, 0.5 * moved, 0.0)
    lower = jnp.where(lane > row + mid, body, 0.0)
    lower = lower + jnp.where(lane == row + mid, 0.5 * diagonal, 0.0)
    once = jnp.concatenate([upper, lower], axis=0)
    return once + once.T


def pairs_kernel(cap, batch, parts, mask, right_mask, *refs):
    inputs, (half, energy, right), scratch = refs[:5], refs[6:9], refs[9:]
    came = refs[5]
    first, shift, occupied, rows, held, turned_over, halves, energies, rights, arrived, left = scratch
    steps, height, width = came.shape
    fit_rows = height - ENERGY_ROWS
    block_count = fit_rows // AUXBLK
    orb_dev = rows.shape[0]
    each = orb_dev // parts

    def own(c):
        slots = pl.ds(c * each, each)
        source = inputs[4].at[slots, pl.ds(0, fit_rows)]
        return pltpu.make_async_copy(source, held.at[slots], arrived.at[4 + c])

    loads = [
        pltpu.make_async_copy(source, target, arrived.at[n])
        for n, (source, target) in enumerate(zip(inputs[:4], (first, shift, occupied, rows)))
    ] + [own(c) for c in range(parts)]
    for load in loads:
        load.start()

    def going(b):
        some = pl.ds(b * batch * cap, batch * cap)
        few = pl.ds((b * batch) ^ (right_mask // batch * batch), batch)
        return (
            pltpu.make_async_copy(halves.at[some], half.at[some], left.at[0, b]),
            pltpu.make_async_copy(energies.at[some], energy.at[some], left.at[1, b]),
            pltpu.make_async_copy(rights.at[few], right.at[few], left.at[2, b]),
        )

    held[orb_dev, :AUXBLK, :] = jnp.zeros((AUXBLK, width), jnp.bfloat16)

    def turn_over(b, carry):
        for u in range(batch):
            turned_over[b * batch + u] = came[b * batch + u, :fit_rows, :].T
        return carry

    lax.fori_loop(0, steps // batch, turn_over, 0)
    for load in loads:
        load.wait()

    def shifted(place):
        moved = []
        for block in range(block_count):
            source = block - shift[place]
            inside = (source >= 0) & (source < block_count)
            slot = jnp.where(inside, first[place], orb_dev)
            begin = pl.multiple_of(jnp.where(inside, source, 0) * AUXBLK, AUXBLK)
            moved.append(held[slot, pl.ds(begin, AUXBLK), :])
        return jnp.concatenate(moved, axis=0)

    def one_batch(b, carry):
        group = [b * batch + u for u in range(batch)]
        couplings, far = [], []
        for step in group:
            side = jnp.concatenate([shifted(step * cap + k) for k in range(cap)], axis=1)
            couplings.append(f32_dot(turned_over[step ^ mask], side, ((1,), (0,))))
            row = came[step ^ mask, fit_rows:, :].astype(jnp.float32)[:1, :]
            far.append(jnp.broadcast_to(row, (width, width)).T)
        for u, step in enumerate(group):
            sides = []
            for k in range(cap):
                place = step * cap + k
                coupling = couplings[u][:, k * width : (k + 1) * width]
                amplitude = coupling / (far[u] + (rows[first[place]] - occupied[place]))
                energies[place] = jnp.sum(coupling * amplitude, axis=0, keepdims=True)
                sides.append(amplitude.astype(jnp.bfloat16))
                halves[place] = sides[-1]
            side = jnp.concatenate(sides, axis=1)
            density = f32_dot(side, side, ((1,), (1,)))
            rights[step ^ right_mask] = fold_symmetric(density).astype(jnp.bfloat16)
        for copy in going(b):
            copy.start()
        return carry

    def finish(b, carry):
        for copy in going(b):
            copy.wait()
        return carry

    lax.fori_loop(0, steps // batch, one_batch, 0)
    lax.fori_loop(0, steps // batch, finish, 0)


def pair_terms(
    mask, right_mask, first, shift, occupied, rows, held, messages, batch=8, parts=8
):
    steps, height, width = messages.shape
    pair_dev = first.shape[0]
    cap = pair_dev // steps
    orb_dev = held.shape[0]
    fit_rows = height - ENERGY_ROWS
    half = (pair_dev, width, width)
    energy = (pair_dev, 1, width)
    right = (steps, width // 2 + DIAGONAL_ROWS, width)
    return pl.pallas_call(
        functools.partial(pairs_kernel, cap, batch, parts, mask, right_mask),
        in_specs=[ANY()] * 5 + [VMEM()],
        out_specs=(ANY(), ANY(), ANY()),
        out_shape=(
            pltpu.HBM(half, jnp.bfloat16),
            pltpu.HBM(energy, jnp.float32),
            pltpu.HBM(right, jnp.bfloat16),
        ),
        scratch_shapes=[
            pltpu.SMEM(first.shape, jnp.int32),
            pltpu.SMEM(shift.shape, jnp.int32),
            pltpu.SMEM(occupied.shape, jnp.float32),
            pltpu.VMEM(rows.shape, jnp.float32),
            pltpu.VMEM((orb_dev + 1, fit_rows, width), jnp.bfloat16),
            pltpu.VMEM((steps, width, fit_rows), jnp.bfloat16),
            pltpu.VMEM(half, jnp.bfloat16),
            pltpu.VMEM(energy, jnp.float32),
            pltpu.VMEM(right, jnp.bfloat16),
            pltpu.SemaphoreType.DMA((4 + parts,)),
            pltpu.SemaphoreType.DMA((3, steps // batch)),
        ],
        compiler_params=pltpu.CompilerParams(vmem_limit_bytes=24 * MIB),
        name="pair_terms",
    )(*map(in_hbm, (first, shift, occupied, rows, held)), messages)


def left_kernel(
    batch, index, first, half, energy, transforms, density, pair_energy, halves, turns, inner, scattered, arrived
):
    orb_dev, width, _ = inner.shape
    pair_dev = half.shape[0]
    loads = [
        pltpu.make_async_copy(half, halves, arrived.at[0]),
        pltpu.make_async_copy(transforms, turns, arrived.at[1]),
    ]
    for load in loads:
        load.start()
    inner[...] = jnp.zeros_like(inner)
    for load in loads:
        load.wait()

    def some_pairs(b, carry):
        places = [b * batch + u for u in range(batch)]
        sums = [f32_dot(halves[place], halves[place], ((0,), (0,))) for place in places]
        for place, one in zip(places, sums):
            slot = first[place]
            inner[slot] = inner[slot] + one
            scattered[index[place]] = energy[place]
        return carry

    lax.fori_loop(0, pair_dev // batch, some_pairs, 0)

    def some_slots(b, carry):
        slots = [b * batch + u for u in range(batch)]
        half_way = [turned(turns[slot], inner[slot]) for slot in slots]
        for slot, one in zip(slots, half_way):
            density[slot] = turned_back(one, turns[slot])
        return carry

    lax.fori_loop(0, orb_dev // batch, some_slots, 0)
    gathered = scattered[...].reshape(pair_dev, width)
    pair_energy[...] = -jnp.sum(gathered.T, axis=0, keepdims=True) / width


def left_density(index, first, half, energy, transforms, batch=8):
    orb_dev = transforms.shape[0]
    pair_dev, width, _ = half.shape
    return pl.pallas_call(
        functools.partial(left_kernel, batch),
        in_specs=[SMEM(), SMEM(), ANY(), VMEM(), ANY()],
        out_specs=(VMEM(), VMEM()),
        out_shape=(
            pltpu.HBM((orb_dev, width, width), jnp.float32),
            pltpu.HBM((1, pair_dev), jnp.float32),
        ),
        scratch_shapes=[
            pltpu.VMEM(half.shape, jnp.bfloat16),
            pltpu.VMEM(transforms.shape, jnp.bfloat16),
            pltpu.VMEM((orb_dev, width, width), jnp.float32),
            pltpu.VMEM((pair_dev, 1, width), jnp.float32),
            pltpu.SemaphoreType.DMA((2,)),
        ],
        compiler_params=pltpu.CompilerParams(vmem_limit_bytes=16 * MIB),
        name="left_density",
    )(*map(in_hbm, (index, first, half, energy, transforms)))


def right_kernel(
    batch, asked_mask, mask, wanted, before, rights, transforms, out, asked, total, parts, turns, arrived, left
):
    senders = rights.shape[0]
    which = pltpu.make_async_copy(wanted, asked, arrived.at[0])
    turns_load = pltpu.make_async_copy(transforms, turns, arrived.at[1])
    total_load = pltpu.make_async_copy(before, total, arrived.at[2])
    for load in (which, turns_load, total_load):
        load.start()

    def unfold(b, carry):
        for u in range(batch):
            full = unfold_symmetric(rights[b * batch + u].astype(jnp.float32))
            parts[b * batch + u] = full.astype(jnp.bfloat16)
        return carry

    lax.fori_loop(0, senders // batch, unfold, 0)
    which.wait()
    turns_load.wait()
    total_load.wait()

    def some_messages(b, carry):
        places = [b * batch + u for u in range(batch)]
        slots = [asked[place ^ mask ^ asked_mask, 0, 0] for place in places]
        half_way = [
            f32_dot(turns[slot], parts[place], ((1,), (0,))) for slot, place in zip(slots, places)
        ]
        sums = [turned_back(one, turns[slot]) for slot, one in zip(slots, half_way)]
        for slot, one in zip(slots, sums):
            total[slot] = total[slot] + one
        return carry

    lax.fori_loop(0, senders // batch, some_messages, 0)

    def going(c):
        slots = pl.ds(c * batch, batch)
        return pltpu.make_async_copy(total.at[slots], out.at[slots], left.at[c])

    for c in range(total.shape[0] // batch):
        going(c).start()
    for c in range(total.shape[0] // batch):
        going(c).wait()


def add_right_density(asked_mask, mask, asked, density, right, transforms, batch=8):
    return pl.pallas_call(
        functools.partial(right_kernel, batch, asked_mask, mask),
        in_specs=[ANY(), ANY(), VMEM(), ANY()],
        out_specs=ANY(),
        out_shape=pltpu.HBM(density.shape, jnp.float32),
        scratch_shapes=[
            pltpu.SMEM(asked.shape, jnp.int32),
            pltpu.VMEM(density.shape, jnp.float32),
            pltpu.VMEM((right.shape[0],) + density.shape[1:], jnp.bfloat16),
            pltpu.VMEM(transforms.shape, jnp.bfloat16),
            pltpu.SemaphoreType.DMA((3,)),
            pltpu.SemaphoreType.DMA((density.shape[0] // batch,)),
        ],
        compiler_params=pltpu.CompilerParams(vmem_limit_bytes=16 * MIB),
        name="add_right_density",
    )(asked, in_hbm(density), right, in_hbm(transforms))


def exchange(messages, mask):
    groups = [[place ^ mask for place in range(messages.shape[0])]]
    return lax.all_to_all(
        messages, "orb", split_axis=0, concat_axis=0, tiled=True, axis_index_groups=groups
    )


def local(pair_list, orbital_slot, blocks, transforms, domain, eps_virt, eps_occ, offsets):
    owners = lax.axis_size("orb")
    orb_dev = blocks.shape[0]
    ask, send, give_back = 3 * owners // 4, owners // 2, 3 * owners // 4
    asked = exchange(wanted_slots(owners, orb_dev, ask, pair_list, orbital_slot), ask)
    rows, held = own_rotated(domain, eps_virt, blocks, transforms)
    incoming = exchange(pack_messages(ask, send, asked, held), send)
    index, first, shift, occupied = plan(
        owners, orb_dev, pair_list, orbital_slot, offsets, eps_occ
    )
    half, energy, right = pair_terms(
        send, give_back, first, shift, occupied, rows, held, incoming
    )
    came_back = exchange(right, give_back)
    density, pair_energy = left_density(index, first, half, energy, transforms)
    density = add_right_density(ask, give_back, asked, density, came_back, transforms)
    return (pair_energy.reshape(-1), density)


def solution(mesh):
    in_specs = (
        P(("groups", "orb"), None),
        P("groups"),
        P(("groups", "orb"), None, None),
        P(("groups", "orb"), None, None),
        P(("groups", "orb"), None),
        P("groups"),
        P("groups"),
        P("groups"),
    )
    out_specs = (P(("groups", "orb")), P(("groups", "orb"), None, None))
    return jax.shard_map(local, mesh=mesh, in_specs=in_specs, out_specs=out_specs, check_vma=False)
```

```python
import functools

import jax
import jax.numpy as jnp
from jax import lax
from jax.experimental import pallas as pl
from jax.experimental.pallas import tpu as pltpu
from jax.sharding import PartitionSpec as P

AUXBLK = 128
ENERGY_ROWS = 16
DIAGONAL_ROWS = 16
MIB = 1024 * 1024

SMEM = functools.partial(pl.BlockSpec, memory_space=pltpu.SMEM)
VMEM = functools.partial(pl.BlockSpec, memory_space=pltpu.VMEM)
ANY = functools.partial(pl.BlockSpec, memory_space=pl.ANY)


def in_hbm(array):
    return pltpu.with_memory_space_constraint(array, pltpu.HBM)


def f32_dot(lhs, rhs, dims):
    return lax.dot_general(lhs, rhs, (dims, ((), ())), preferred_element_type=jnp.float32)


def in_two_parts(value):
    high = value.astype(jnp.bfloat16)
    return high, (value - high.astype(jnp.float32)).astype(jnp.bfloat16)


def turned(turn, inner):
    width = inner.shape[1]
    both = f32_dot(turn, jnp.concatenate(in_two_parts(inner), axis=1), ((1,), (0,)))
    return both[:, :width] + both[:, width:]


def turned_back(half_way, turn):
    height = half_way.shape[0]
    both = f32_dot(jnp.concatenate(in_two_parts(half_way), axis=0), turn, ((1,), (1,)))
    return both[:height] + both[height:]


def wanted_kernel(orb_dev, mask, pairs, slots, wanted):
    def one_pair(pair, carry):
        slot = slots[pairs[1, pair]]
        owner = lax.div(slot, jnp.int32(orb_dev))
        local_slot = lax.rem(slot, jnp.int32(orb_dev))
        wanted[owner ^ mask] = jnp.full(wanted.shape[1:], local_slot, jnp.int32)
        return carry

    lax.fori_loop(0, pairs.shape[1], one_pair, 0, unroll=16)


def wanted_slots(owners, orb_dev, mask, pair_list, orbital_slot):
    return pl.pallas_call(
        functools.partial(wanted_kernel, orb_dev, mask),
        out_shape=pltpu.HBM((owners, 1, 128), jnp.int32),
        in_specs=[SMEM()] * 2,
        out_specs=VMEM(),
        name="wanted_slots",
    )(*map(in_hbm, (pair_list.T, orbital_slot)))


def plan_kernel(orb_dev, cap, pairs, slots, offsets, eps_occ, index, first, shift, occupied, seen):
    owners = seen.shape[0]

    def clear(owner, carry):
        seen[owner] = 0
        return carry

    lax.fori_loop(0, owners, clear, 0, unroll=8)

    def one_pair(pair, carry):
        slot_i = slots[pairs[0, pair]]
        slot_j = slots[pairs[1, pair]]
        owner = lax.div(slot_j, jnp.int32(orb_dev))
        rank = seen[owner]
        seen[owner] = rank + 1
        place = owner * cap + rank
        index[place] = pair
        first[place] = lax.rem(slot_i, jnp.int32(orb_dev))
        shift[place] = offsets[slot_i] - offsets[slot_j]
        occupied[place] = eps_occ[slot_i] + eps_occ[slot_j]
        return carry

    lax.fori_loop(0, pairs.shape[1], one_pair, 0, unroll=8)


def plan(owners, orb_dev, pair_list, orbital_slot, offsets, eps_occ):
    pair_dev = pair_list.shape[0]
    cap = pair_dev // owners
    sorted_ints = pltpu.HBM((pair_dev,), jnp.int32)
    return pl.pallas_call(
        functools.partial(plan_kernel, orb_dev, cap),
        out_shape=(
            sorted_ints,
            sorted_ints,
            sorted_ints,
            pltpu.HBM((pair_dev,), jnp.float32),
        ),
        in_specs=[SMEM()] * 4,
        out_specs=(SMEM(), SMEM(), SMEM(), SMEM()),
        scratch_shapes=[pltpu.SMEM((owners,), jnp.int32)],
        name="plan",
    )(*map(in_hbm, (pair_list.T, orbital_slot, offsets, eps_occ)))


def own_kernel(
    chunk, domain, eps_virt, blocks, transforms, rows, held, wanted, table, found, block_rows, turns, made, arrived, left
):
    orb_dev, fit_rows, width = blocks.shape
    chunks = orb_dev // chunk

    def coming(c):
        part = pl.ds(c * chunk, chunk)
        return (
            pltpu.make_async_copy(blocks.at[part], block_rows.at[part], arrived.at[0, c]),
            pltpu.make_async_copy(transforms.at[part], turns.at[part], arrived.at[1, c]),
        )

    def going(c):
        part = pl.ds(c * chunk, chunk)
        return pltpu.make_async_copy(made.at[part], held.at[part], left.at[c])

    loads = [
        pltpu.make_async_copy(domain, wanted, arrived.at[0, chunks]),
        pltpu.make_async_copy(eps_virt, table, arrived.at[1, chunks]),
    ]
    for load in loads:
        load.start()
    for c in range(chunks):
        for copy in coming(c):
            copy.start()
    for load in loads:
        load.wait()
    line, lane = wanted[...] // 128, wanted[...] % 128
    energies = jnp.zeros((orb_dev, width), jnp.float32)
    for k in range(table.shape[0]):
        spread = jnp.broadcast_to(table[pl.ds(k, 1), :], (orb_dev, width))
        picked = jnp.take_along_axis(spread, lane, axis=1)
        energies = jnp.where(line == k, picked, energies)
    rounded = energies.astype(jnp.bfloat16).astype(jnp.float32)
    for s in range(orb_dev):
        row = rounded[s : s + 1, :]
        found[s] = row
        made[s, fit_rows:, :] = jnp.broadcast_to(row, (ENERGY_ROWS, width)).astype(jnp.bfloat16)
    rows_out = pltpu.make_async_copy(found, rows, left.at[chunks])
    rows_out.start()

    def one_chunk(c, carry):
        for copy in coming(c):
            copy.wait()
        slots = [c * chunk + u for u in range(chunk)]
        rotated = [f32_dot(block_rows[slot], turns[slot], ((1,), (0,))) for slot in slots]
        for slot, one in zip(slots, rotated):
            made[slot, :fit_rows, :] = one.astype(jnp.bfloat16)
        going(c).start()
        return carry

    lax.fori_loop(0, chunks, one_chunk, 0)
    rows_out.wait()
    for c in range(chunks):
        going(c).wait()


def own_rotated(domain, eps_virt, blocks, transforms, chunk=4):
    orb_dev, fit_rows, width = blocks.shape
    shape = (orb_dev, fit_rows + ENERGY_ROWS, width)
    table = (eps_virt.shape[0] // 128, 128)
    return pl.pallas_call(
        functools.partial(own_kernel, chunk),
        in_specs=[ANY()] * 4,
        out_specs=(ANY(), ANY()),
        out_shape=(
            pltpu.HBM((orb_dev, 1, width), jnp.float32),
            pltpu.HBM(shape, jnp.bfloat16),
        ),
        scratch_shapes=[
            pltpu.VMEM(domain.shape, jnp.int32),
            pltpu.VMEM(table, jnp.float32),
            pltpu.VMEM((orb_dev, 1, width), jnp.float32),
            pltpu.VMEM(blocks.shape, jnp.bfloat16),
            pltpu.VMEM(transforms.shape, jnp.bfloat16),
            pltpu.VMEM(shape, jnp.bfloat16),
            pltpu.SemaphoreType.DMA((2, orb_dev // chunk + 1)),
            pltpu.SemaphoreType.DMA((orb_dev // chunk + 1,)),
        ],
        compiler_params=pltpu.CompilerParams(vmem_limit_bytes=16 * MIB),
        name="own_rotated",
    )(*map(in_hbm, (domain, eps_virt.reshape(table), blocks, transforms)))


def pack_kernel(asked_mask, mask, asked, held, messages, made, arrived, left):
    owners = messages.shape[0]

    def coming(owner):
        source = held.at[asked[owner ^ asked_mask, 0, 0]]
        return pltpu.make_async_copy(source, made.at[owner], arrived.at[owner])

    def going(owner):
        return pltpu.make_async_copy(made.at[owner], messages.at[owner ^ mask], left.at[owner])

    def start(owner, carry):
        coming(owner).start()
        return carry

    def forward(owner, carry):
        coming(owner).wait()
        going(owner).start()
        return carry

    def finish(owner, carry):
        going(owner).wait()
        return carry

    for step in (start, forward, finish):
        lax.fori_loop(0, owners, step, 0, unroll=4)


def pack_messages(asked_mask, mask, asked, held):
    owners = asked.shape[0]
    shape = (owners,) + held.shape[1:]
    return pl.pallas_call(
        functools.partial(pack_kernel, asked_mask, mask),
        in_specs=[SMEM(), ANY()],
        out_specs=ANY(),
        out_shape=pltpu.HBM(shape, jnp.bfloat16),
        scratch_shapes=[
            pltpu.VMEM(shape, jnp.bfloat16),
            pltpu.SemaphoreType.DMA((owners,)),
            pltpu.SemaphoreType.DMA((owners,)),
        ],
        compiler_params=pltpu.CompilerParams(vmem_limit_bytes=16 * MIB),
        name="pack_messages",
    )(asked, in_hbm(held))


def fold_symmetric(full):
    width = full.shape[0]
    mid = width // 2
    row = lax.broadcasted_iota(jnp.int32, (mid, width), 0)
    lane = lax.broadcasted_iota(jnp.int32, (mid, width), 1)
    upper, lower = full[:mid, :], full[mid:, :]
    folded = jnp.where(lane <= row + mid, pltpu.roll(upper, mid, 1), lower)
    diagonal = jnp.sum(jnp.where(lane == row + mid, lower, 0.0), axis=0, keepdims=True)
    return jnp.concatenate([folded, jnp.broadcast_to(diagonal, (DIAGONAL_ROWS, width))], axis=0)


def unfold_symmetric(folded):
    width = folded.shape[1]
    mid = width // 2
    row = lax.broadcasted_iota(jnp.int32, (mid, width), 0)
    lane = lax.broadcasted_iota(jnp.int32, (mid, width), 1)
    body, diagonal = folded[:mid, :], folded[mid : mid + 1, :]
    moved = pltpu.roll(body, mid, 1)
    upper = jnp.where(lane < row, moved, 0.0) + jnp.where(lane >= mid, moved, 0.0)
    upper = upper + jnp.where(lane == row, 0.5 * moved, 0.0)
    lower = jnp.where(lane > row + mid, body, 0.0)
    lower = lower + jnp.where(lane == row + mid, 0.5 * diagonal, 0.0)
    once = jnp.concatenate([upper, lower], axis=0)
    return once + once.T


def pairs_kernel(cap, batch, parts, mask, right_mask, *refs):
    inputs, (half, energy, right), scratch = refs[:5], refs[6:9], refs[9:]
    came = refs[5]
    first, shift, occupied, rows, held, turned_over, halves, energies, rights, arrived, left = scratch
    steps, height, width = came.shape
    fit_rows = height - ENERGY_ROWS
    block_count = fit_rows // AUXBLK
    orb_dev = rows.shape[0]
    each = orb_dev // parts

    def own(c):
        slots = pl.ds(c * each, each)
        source = inputs[4].at[slots, pl.ds(0, fit_rows)]
        return pltpu.make_async_copy(source, held.at[slots], arrived.at[4 + c])

    loads = [
        pltpu.make_async_copy(source, target, arrived.at[n])
        for n, (source, target) in enumerate(zip(inputs[:4], (first, shift, occupied, rows)))
    ] + [own(c) for c in range(parts)]
    for load in loads:
        load.start()

    def going(b):
        some = pl.ds(b * batch * cap, batch * cap)
        few = pl.ds((b * batch) ^ (right_mask // batch * batch), batch)
        return (
            pltpu.make_async_copy(halves.at[some], half.at[some], left.at[0, b]),
            pltpu.make_async_copy(energies.at[some], energy.at[some], left.at[1, b]),
            pltpu.make_async_copy(rights.at[few], right.at[few], left.at[2, b]),
        )

    held[orb_dev, :AUXBLK, :] = jnp.zeros((AUXBLK, width), jnp.bfloat16)

    def turn_over(b, carry):
        for u in range(batch):
            turned_over[b * batch + u] = came[b * batch + u, :fit_rows, :].T
        return carry

    lax.fori_loop(0, steps // batch, turn_over, 0)
    for load in loads:
        load.wait()

    def shifted(place):
        moved = []
        for block in range(block_count):
            source = block - shift[place]
            inside = (source >= 0) & (source < block_count)
            slot = jnp.where(inside, first[place], orb_dev)
            begin = pl.multiple_of(jnp.where(inside, source, 0) * AUXBLK, AUXBLK)
            moved.append(held[slot, pl.ds(begin, AUXBLK), :])
        return jnp.concatenate(moved, axis=0)

    def one_batch(b, carry):
        group = [b * batch + u for u in range(batch)]
        couplings, far = [], []
        for step in group:
            side = jnp.concatenate([shifted(step * cap + k) for k in range(cap)], axis=1)
            couplings.append(f32_dot(turned_over[step ^ mask], side, ((1,), (0,))))
            row = came[step ^ mask, fit_rows:, :].astype(jnp.float32)[:1, :]
            far.append(jnp.broadcast_to(row, (width, width)).T)
        for u, step in enumerate(group):
            sides = []
            for k in range(cap):
                place = step * cap + k
                coupling = couplings[u][:, k * width : (k + 1) * width]
                amplitude = coupling / (far[u] + (rows[first[place]] - occupied[place]))
                energies[place] = jnp.sum(coupling * amplitude, axis=0, keepdims=True)
                sides.append(amplitude.astype(jnp.bfloat16))
                halves[place] = sides[-1]
            side = jnp.concatenate(sides, axis=1)
            density = f32_dot(side, side, ((1,), (1,)))
            rights[step ^ right_mask] = fold_symmetric(density).astype(jnp.bfloat16)
        for copy in going(b):
            copy.start()
        return carry

    def finish(b, carry):
        for copy in going(b):
            copy.wait()
        return carry

    lax.fori_loop(0, steps // batch, one_batch, 0)
    lax.fori_loop(0, steps // batch, finish, 0)


def pair_terms(
    mask, right_mask, first, shift, occupied, rows, held, messages, batch=8, parts=8
):
    steps, height, width = messages.shape
    pair_dev = first.shape[0]
    cap = pair_dev // steps
    orb_dev = held.shape[0]
    fit_rows = height - ENERGY_ROWS
    half = (pair_dev, width, width)
    energy = (pair_dev, 1, width)
    right = (steps, width // 2 + DIAGONAL_ROWS, width)
    return pl.pallas_call(
        functools.partial(pairs_kernel, cap, batch, parts, mask, right_mask),
        in_specs=[ANY()] * 5 + [VMEM()],
        out_specs=(ANY(), ANY(), ANY()),
        out_shape=(
            pltpu.HBM(half, jnp.bfloat16),
            pltpu.HBM(energy, jnp.float32),
            pltpu.HBM(right, jnp.bfloat16),
        ),
        scratch_shapes=[
            pltpu.SMEM(first.shape, jnp.int32),
            pltpu.SMEM(shift.shape, jnp.int32),
            pltpu.SMEM(occupied.shape, jnp.float32),
            pltpu.VMEM(rows.shape, jnp.float32),
            pltpu.VMEM((orb_dev + 1, fit_rows, width), jnp.bfloat16),
            pltpu.VMEM((steps, width, fit_rows), jnp.bfloat16),
            pltpu.VMEM(half, jnp.bfloat16),
            pltpu.VMEM(energy, jnp.float32),
            pltpu.VMEM(right, jnp.bfloat16),
            pltpu.SemaphoreType.DMA((4 + parts,)),
            pltpu.SemaphoreType.DMA((3, steps // batch)),
        ],
        compiler_params=pltpu.CompilerParams(vmem_limit_bytes=24 * MIB),
        name="pair_terms",
    )(*map(in_hbm, (first, shift, occupied, rows, held)), messages)


def left_kernel(batch, *refs):
    inputs, (density, pair_energy), scratch = refs[:5], refs[5:7], refs[7:]
    index, first, energy, halves, turns, inner, scattered, made, energies, arrived, left = scratch
    orb_dev, width, _ = inner.shape
    pair_dev = halves.shape[0]
    parts = pair_dev // batch

    def half(b):
        some = pl.ds(b * batch, batch)
        return pltpu.make_async_copy(inputs[3].at[some], halves.at[some], arrived.at[4 + b])

    def going(b):
        some = pl.ds(b * batch, batch)
        return pltpu.make_async_copy(made.at[some], density.at[some], left.at[b])

    loads = [
        pltpu.make_async_copy(inputs[n], target, arrived.at[n])
        for n, target in enumerate((index, first, energy))
    ]
    turns_load = pltpu.make_async_copy(inputs[4], turns, arrived.at[3])
    for load in loads:
        load.start()
    for b in range(parts):
        half(b).start()
    turns_load.start()
    inner[...] = jnp.zeros_like(inner)
    for load in loads:
        load.wait()

    def scatter(place, carry):
        scattered[index[place]] = energy[place]
        return carry

    lax.fori_loop(0, pair_dev, scatter, 0, unroll=8)
    gathered = scattered[...].reshape(pair_dev, width)
    energies[...] = -jnp.sum(gathered.T, axis=0, keepdims=True) / width
    energies_out = pltpu.make_async_copy(energies, pair_energy, left.at[orb_dev // batch])
    energies_out.start()

    def some_pairs(b, carry):
        half(b).wait()
        places = [b * batch + u for u in range(batch)]
        sums = [f32_dot(halves[place], halves[place], ((0,), (0,))) for place in places]
        for place, one in zip(places, sums):
            slot = first[place]
            inner[slot] = inner[slot] + one
        return carry

    lax.fori_loop(0, parts, some_pairs, 0)
    turns_load.wait()

    def some_slots(b, carry):
        slots = [b * batch + u for u in range(batch)]
        half_way = [turned(turns[slot], inner[slot]) for slot in slots]
        for slot, one in zip(slots, half_way):
            made[slot] = turned_back(one, turns[slot])
        going(b).start()
        return carry

    lax.fori_loop(0, orb_dev // batch, some_slots, 0)
    energies_out.wait()
    for b in range(orb_dev // batch):
        going(b).wait()


def left_density(index, first, energy, half, transforms, batch=8):
    orb_dev = transforms.shape[0]
    pair_dev, width, _ = half.shape
    density = (orb_dev, width, width)
    return pl.pallas_call(
        functools.partial(left_kernel, batch),
        in_specs=[ANY()] * 5,
        out_specs=(ANY(), ANY()),
        out_shape=(pltpu.HBM(density, jnp.float32), pltpu.HBM((1, pair_dev), jnp.float32)),
        scratch_shapes=[
            pltpu.SMEM(index.shape, jnp.int32),
            pltpu.SMEM(first.shape, jnp.int32),
            pltpu.VMEM(energy.shape, jnp.float32),
            pltpu.VMEM(half.shape, jnp.bfloat16),
            pltpu.VMEM(transforms.shape, jnp.bfloat16),
            pltpu.VMEM(density, jnp.float32),
            pltpu.VMEM(energy.shape, jnp.float32),
            pltpu.VMEM(density, jnp.float32),
            pltpu.VMEM((1, pair_dev), jnp.float32),
            pltpu.SemaphoreType.DMA((4 + pair_dev // batch,)),
            pltpu.SemaphoreType.DMA((orb_dev // batch + 1,)),
        ],
        compiler_params=pltpu.CompilerParams(vmem_limit_bytes=16 * MIB),
        name="left_density",
    )(*map(in_hbm, (index, first, energy, half, transforms)))


def right_kernel(
    batch, parts, asked_mask, mask, wanted, before, rights, transforms, out, asked, total, unfolded, turns, arrived, left
):
    senders = rights.shape[0]
    each = total.shape[0] // parts
    chunks = [pl.ds(c * each, each) for c in range(parts)]
    loads = [pltpu.make_async_copy(wanted, asked, arrived.at[0, parts])]
    for n, (source, target) in enumerate(((transforms, turns), (before, total))):
        for c, chunk in enumerate(chunks):
            loads.append(
                pltpu.make_async_copy(source.at[chunk], target.at[chunk], arrived.at[n, c])
            )
    for load in loads:
        load.start()

    def unfold(b, carry):
        for u in range(batch):
            full = unfold_symmetric(rights[b * batch + u].astype(jnp.float32))
            unfolded[b * batch + u] = full.astype(jnp.bfloat16)
        return carry

    lax.fori_loop(0, senders // batch, unfold, 0)
    for load in loads:
        load.wait()

    def some_messages(b, carry):
        places = [b * batch + u for u in range(batch)]
        slots = [asked[place ^ mask ^ asked_mask, 0, 0] for place in places]
        half_way = [
            f32_dot(turns[slot], unfolded[place], ((1,), (0,)))
            for slot, place in zip(slots, places)
        ]
        sums = [turned_back(one, turns[slot]) for slot, one in zip(slots, half_way)]
        for slot, one in zip(slots, sums):
            total[slot] = total[slot] + one
        return carry

    lax.fori_loop(0, senders // batch, some_messages, 0)

    stores = [
        pltpu.make_async_copy(total.at[chunk], out.at[chunk], left.at[c])
        for c, chunk in enumerate(chunks)
    ]
    for store in stores:
        store.start()
    for store in stores:
        store.wait()


def add_right_density(asked_mask, mask, asked, density, right, transforms, batch=16, parts=4):
    return pl.pallas_call(
        functools.partial(right_kernel, batch, parts, asked_mask, mask),
        in_specs=[ANY(), ANY(), VMEM(), ANY()],
        out_specs=ANY(),
        out_shape=pltpu.HBM(density.shape, jnp.float32),
        scratch_shapes=[
            pltpu.SMEM(asked.shape, jnp.int32),
            pltpu.VMEM(density.shape, jnp.float32),
            pltpu.VMEM((right.shape[0],) + density.shape[1:], jnp.bfloat16),
            pltpu.VMEM(transforms.shape, jnp.bfloat16),
            pltpu.SemaphoreType.DMA((2, parts + 1)),
            pltpu.SemaphoreType.DMA((parts,)),
        ],
        compiler_params=pltpu.CompilerParams(vmem_limit_bytes=16 * MIB),
        name="add_right_density",
    )(asked, in_hbm(density), right, in_hbm(transforms))


def exchange(messages, mask):
    groups = [[place ^ mask for place in range(messages.shape[0])]]
    return lax.all_to_all(
        messages, "orb", split_axis=0, concat_axis=0, tiled=True, axis_index_groups=groups
    )


def local(pair_list, orbital_slot, blocks, transforms, domain, eps_virt, eps_occ, offsets):
    owners = lax.axis_size("orb")
    orb_dev = blocks.shape[0]
    ask, send, give_back = owners // 2, owners // 2, 3 * owners // 4
    asked = exchange(wanted_slots(owners, orb_dev, ask, pair_list, orbital_slot), ask)
    rows, held = own_rotated(domain, eps_virt, blocks, transforms)
    incoming = exchange(pack_messages(ask, send, asked, held), send)
    index, first, shift, occupied = plan(
        owners, orb_dev, pair_list, orbital_slot, offsets, eps_occ
    )
    half, energy, right = pair_terms(
        send, give_back, first, shift, occupied, rows, held, incoming
    )
    came_back = exchange(right, give_back)
    density, pair_energy = left_density(index, first, energy, half, transforms)
    density = add_right_density(ask, give_back, asked, density, came_back, transforms)
    return (pair_energy.reshape(-1), density)


def solution(mesh):
    in_specs = (
        P(("groups", "orb"), None),
        P("groups"),
        P(("groups", "orb"), None, None),
        P(("groups", "orb"), None, None),
        P(("groups", "orb"), None),
        P("groups"),
        P("groups"),
        P("groups"),
    )
    out_specs = (P(("groups", "orb")), P(("groups", "orb"), None, None))
    return jax.shard_map(local, mesh=mesh, in_specs=in_specs, out_specs=out_specs, check_vma=False)
```

```python
import functools

import jax
import jax.numpy as jnp
from jax import lax
from jax.experimental import pallas as pl
from jax.experimental.pallas import tpu as pltpu
from jax.sharding import PartitionSpec as P

AUXBLK = 128
ENERGY_ROWS = 16
DIAGONAL_ROWS = 16
MIB = 1024 * 1024

SMEM = functools.partial(pl.BlockSpec, memory_space=pltpu.SMEM)
VMEM = functools.partial(pl.BlockSpec, memory_space=pltpu.VMEM)
ANY = functools.partial(pl.BlockSpec, memory_space=pl.ANY)


def in_hbm(array):
    return pltpu.with_memory_space_constraint(array, pltpu.HBM)


def f32_dot(lhs, rhs, dims):
    return lax.dot_general(lhs, rhs, (dims, ((), ())), preferred_element_type=jnp.float32)


def in_two_parts(value):
    high = value.astype(jnp.bfloat16)
    return high, (value - high.astype(jnp.float32)).astype(jnp.bfloat16)


def turned(turn, inner):
    width = inner.shape[1]
    both = f32_dot(turn, jnp.concatenate(in_two_parts(inner), axis=1), ((1,), (0,)))
    return both[:, :width] + both[:, width:]


def turned_back(half_way, turn):
    height = half_way.shape[0]
    both = f32_dot(jnp.concatenate(in_two_parts(half_way), axis=0), turn, ((1,), (1,)))
    return both[:height] + both[height:]


def wanted_kernel(orb_dev, mask, pairs, slots, wanted):
    def one_pair(pair, carry):
        slot = slots[pairs[1, pair]]
        owner = lax.div(slot, jnp.int32(orb_dev))
        local_slot = lax.rem(slot, jnp.int32(orb_dev))
        wanted[owner ^ mask] = jnp.full(wanted.shape[1:], local_slot, jnp.int32)
        return carry

    lax.fori_loop(0, pairs.shape[1], one_pair, 0, unroll=16)


def wanted_slots(owners, orb_dev, mask, pair_list, orbital_slot):
    return pl.pallas_call(
        functools.partial(wanted_kernel, orb_dev, mask),
        out_shape=pltpu.HBM((owners, 1, 128), jnp.int32),
        in_specs=[SMEM()] * 2,
        out_specs=VMEM(),
        name="wanted_slots",
    )(*map(in_hbm, (pair_list.T, orbital_slot)))


def plan_kernel(orb_dev, cap, pairs, slots, offsets, eps_occ, index, first, shift, occupied, seen):
    owners = seen.shape[0]

    def clear(owner, carry):
        seen[owner] = 0
        return carry

    lax.fori_loop(0, owners, clear, 0, unroll=8)

    def one_pair(pair, carry):
        slot_i = slots[pairs[0, pair]]
        slot_j = slots[pairs[1, pair]]
        owner = lax.div(slot_j, jnp.int32(orb_dev))
        rank = seen[owner]
        seen[owner] = rank + 1
        place = owner * cap + rank
        index[place] = pair
        first[place] = lax.rem(slot_i, jnp.int32(orb_dev))
        shift[place] = offsets[slot_i] - offsets[slot_j]
        occupied[place] = eps_occ[slot_i] + eps_occ[slot_j]
        return carry

    lax.fori_loop(0, pairs.shape[1], one_pair, 0, unroll=8)


def plan(owners, orb_dev, pair_list, orbital_slot, offsets, eps_occ):
    pair_dev = pair_list.shape[0]
    cap = pair_dev // owners
    sorted_ints = pltpu.HBM((pair_dev,), jnp.int32)
    return pl.pallas_call(
        functools.partial(plan_kernel, orb_dev, cap),
        out_shape=(
            sorted_ints,
            sorted_ints,
            sorted_ints,
            pltpu.HBM((pair_dev,), jnp.float32),
        ),
        in_specs=[SMEM()] * 4,
        out_specs=(SMEM(), SMEM(), SMEM(), SMEM()),
        scratch_shapes=[pltpu.SMEM((owners,), jnp.int32)],
        name="plan",
    )(*map(in_hbm, (pair_list.T, orbital_slot, offsets, eps_occ)))


def own_kernel(
    chunk, domain, eps_virt, blocks, transforms, rows, held, wanted, table, found, block_rows, turns, made, arrived, left
):
    orb_dev, fit_rows, width = blocks.shape
    chunks = orb_dev // chunk

    def coming(c):
        part = pl.ds(c * chunk, chunk)
        return (
            pltpu.make_async_copy(blocks.at[part], block_rows.at[part], arrived.at[0, c]),
            pltpu.make_async_copy(transforms.at[part], turns.at[part], arrived.at[1, c]),
        )

    def going(c):
        part = pl.ds(c * chunk, chunk)
        return pltpu.make_async_copy(made.at[part], held.at[part], left.at[c])

    loads = [
        pltpu.make_async_copy(domain, wanted, arrived.at[0, chunks]),
        pltpu.make_async_copy(eps_virt, table, arrived.at[1, chunks]),
    ]
    for load in loads:
        load.start()
    for c in range(chunks):
        for copy in coming(c):
            copy.start()
    for load in loads:
        load.wait()
    line, lane = wanted[...] // 128, wanted[...] % 128
    energies = jnp.zeros((orb_dev, width), jnp.float32)
    for k in range(table.shape[0]):
        spread = jnp.broadcast_to(table[pl.ds(k, 1), :], (orb_dev, width))
        picked = jnp.take_along_axis(spread, lane, axis=1)
        energies = jnp.where(line == k, picked, energies)
    rounded = energies.astype(jnp.bfloat16).astype(jnp.float32)
    for s in range(orb_dev):
        row = rounded[s : s + 1, :]
        found[s] = row
        made[s, fit_rows:, :] = jnp.broadcast_to(row, (ENERGY_ROWS, width)).astype(jnp.bfloat16)
    rows_out = pltpu.make_async_copy(found, rows, left.at[chunks])
    rows_out.start()

    def one_chunk(c, carry):
        for copy in coming(c):
            copy.wait()
        slots = [c * chunk + u for u in range(chunk)]
        rotated = [f32_dot(block_rows[slot], turns[slot], ((1,), (0,))) for slot in slots]
        for slot, one in zip(slots, rotated):
            made[slot, :fit_rows, :] = one.astype(jnp.bfloat16)
        going(c).start()
        return carry

    lax.fori_loop(0, chunks, one_chunk, 0)
    rows_out.wait()
    for c in range(chunks):
        going(c).wait()


def own_rotated(domain, eps_virt, blocks, transforms, chunk=4):
    orb_dev, fit_rows, width = blocks.shape
    shape = (orb_dev, fit_rows + ENERGY_ROWS, width)
    table = (eps_virt.shape[0] // 128, 128)
    return pl.pallas_call(
        functools.partial(own_kernel, chunk),
        in_specs=[ANY()] * 4,
        out_specs=(ANY(), ANY()),
        out_shape=(
            pltpu.HBM((orb_dev, 1, width), jnp.float32),
            pltpu.HBM(shape, jnp.bfloat16),
        ),
        scratch_shapes=[
            pltpu.VMEM(domain.shape, jnp.int32),
            pltpu.VMEM(table, jnp.float32),
            pltpu.VMEM((orb_dev, 1, width), jnp.float32),
            pltpu.VMEM(blocks.shape, jnp.bfloat16),
            pltpu.VMEM(transforms.shape, jnp.bfloat16),
            pltpu.VMEM(shape, jnp.bfloat16),
            pltpu.SemaphoreType.DMA((2, orb_dev // chunk + 1)),
            pltpu.SemaphoreType.DMA((orb_dev // chunk + 1,)),
        ],
        compiler_params=pltpu.CompilerParams(vmem_limit_bytes=16 * MIB),
        name="own_rotated",
    )(*map(in_hbm, (domain, eps_virt.reshape(table), blocks, transforms)))


def pack_kernel(asked_mask, mask, asked, held, messages, made, arrived, left):
    owners = messages.shape[0]

    def coming(owner):
        source = held.at[asked[owner ^ asked_mask, 0, 0]]
        return pltpu.make_async_copy(source, made.at[owner], arrived.at[owner])

    def going(owner):
        return pltpu.make_async_copy(made.at[owner], messages.at[owner ^ mask], left.at[owner])

    def start(owner, carry):
        coming(owner).start()
        return carry

    def forward(owner, carry):
        coming(owner).wait()
        going(owner).start()
        return carry

    def finish(owner, carry):
        going(owner).wait()
        return carry

    for step in (start, forward, finish):
        lax.fori_loop(0, owners, step, 0, unroll=4)


def pack_messages(asked_mask, mask, asked, held):
    owners = asked.shape[0]
    shape = (owners,) + held.shape[1:]
    return pl.pallas_call(
        functools.partial(pack_kernel, asked_mask, mask),
        in_specs=[SMEM(), ANY()],
        out_specs=ANY(),
        out_shape=pltpu.HBM(shape, jnp.bfloat16),
        scratch_shapes=[
            pltpu.VMEM(shape, jnp.bfloat16),
            pltpu.SemaphoreType.DMA((owners,)),
            pltpu.SemaphoreType.DMA((owners,)),
        ],
        compiler_params=pltpu.CompilerParams(vmem_limit_bytes=16 * MIB),
        name="pack_messages",
    )(asked, in_hbm(held))


def fold_symmetric(full):
    width = full.shape[0]
    mid = width // 2
    row = lax.broadcasted_iota(jnp.int32, (mid, width), 0)
    lane = lax.broadcasted_iota(jnp.int32, (mid, width), 1)
    upper, lower = full[:mid, :], full[mid:, :]
    folded = jnp.where(lane <= row + mid, pltpu.roll(upper, mid, 1), lower)
    diagonal = jnp.sum(jnp.where(lane == row + mid, lower, 0.0), axis=0, keepdims=True)
    return jnp.concatenate([folded, jnp.broadcast_to(diagonal, (DIAGONAL_ROWS, width))], axis=0)


def unfold_symmetric(folded):
    width = folded.shape[1]
    mid = width // 2
    row = lax.broadcasted_iota(jnp.int32, (mid, width), 0)
    lane = lax.broadcasted_iota(jnp.int32, (mid, width), 1)
    body, diagonal = folded[:mid, :], folded[mid : mid + 1, :]
    moved = pltpu.roll(body, mid, 1)
    upper = jnp.where(lane < row, moved, 0.0) + jnp.where(lane >= mid, moved, 0.0)
    upper = upper + jnp.where(lane == row, 0.5 * moved, 0.0)
    lower = jnp.where(lane > row + mid, body, 0.0)
    lower = lower + jnp.where(lane == row + mid, 0.5 * diagonal, 0.0)
    once = jnp.concatenate([upper, lower], axis=0)
    return once + once.T


def pairs_kernel(cap, batch, parts, mask, right_mask, *refs):
    inputs, (half, energy, right), scratch = refs[:5], refs[6:9], refs[9:]
    came = refs[5]
    first, shift, occupied, rows, held, turned_over, halves, energies, rights, arrived, left = scratch
    steps, height, width = came.shape
    fit_rows = height - ENERGY_ROWS
    block_count = fit_rows // AUXBLK
    orb_dev = rows.shape[0]
    each = orb_dev // parts

    def own(c):
        slots = pl.ds(c * each, each)
        source = inputs[4].at[slots, pl.ds(0, fit_rows)]
        return pltpu.make_async_copy(source, held.at[slots], arrived.at[4 + c])

    loads = [
        pltpu.make_async_copy(source, target, arrived.at[n])
        for n, (source, target) in enumerate(zip(inputs[:4], (first, shift, occupied, rows)))
    ] + [own(c) for c in range(parts)]
    for load in loads:
        load.start()

    def going(b):
        some = pl.ds(b * batch * cap, batch * cap)
        few = pl.ds((b * batch) ^ (right_mask // batch * batch), batch)
        return (
            pltpu.make_async_copy(halves.at[some], half.at[some], left.at[0, b]),
            pltpu.make_async_copy(energies.at[some], energy.at[some], left.at[1, b]),
            pltpu.make_async_copy(rights.at[few], right.at[few], left.at[2, b]),
        )

    held[orb_dev, :AUXBLK, :] = jnp.zeros((AUXBLK, width), jnp.bfloat16)

    def turn_over(b, carry):
        for u in range(batch):
            turned_over[b * batch + u] = came[b * batch + u, :fit_rows, :].T
        return carry

    lax.fori_loop(0, steps // batch, turn_over, 0)
    for load in loads:
        load.wait()

    def shifted(place):
        moved = []
        for block in range(block_count):
            source = block - shift[place]
            inside = (source >= 0) & (source < block_count)
            slot = jnp.where(inside, first[place], orb_dev)
            begin = pl.multiple_of(jnp.where(inside, source, 0) * AUXBLK, AUXBLK)
            moved.append(held[slot, pl.ds(begin, AUXBLK), :])
        return jnp.concatenate(moved, axis=0)

    def one_batch(b, carry):
        group = [b * batch + u for u in range(batch)]
        couplings, far = [], []
        for step in group:
            side = jnp.concatenate([shifted(step * cap + k) for k in range(cap)], axis=1)
            couplings.append(f32_dot(turned_over[step ^ mask], side, ((1,), (0,))))
            row = came[step ^ mask, fit_rows:, :].astype(jnp.float32)[:1, :]
            far.append(jnp.broadcast_to(row, (width, width)).T)
        for u, step in enumerate(group):
            sides = []
            for k in range(cap):
                place = step * cap + k
                coupling = couplings[u][:, k * width : (k + 1) * width]
                amplitude = coupling / (far[u] + (rows[first[place]] - occupied[place]))
                energies[place] = jnp.sum(coupling * amplitude, axis=0, keepdims=True)
                sides.append(amplitude.astype(jnp.bfloat16))
                halves[place] = sides[-1]
            side = jnp.concatenate(sides, axis=1)
            density = f32_dot(side, side, ((1,), (1,)))
            rights[step ^ right_mask] = fold_symmetric(density).astype(jnp.bfloat16)
        for copy in going(b):
            copy.start()
        return carry

    def finish(b, carry):
        for copy in going(b):
            copy.wait()
        return carry

    lax.fori_loop(0, steps // batch, one_batch, 0)
    lax.fori_loop(0, steps // batch, finish, 0)


def pair_terms(
    mask, right_mask, first, shift, occupied, rows, held, messages, batch=8, parts=8
):
    steps, height, width = messages.shape
    pair_dev = first.shape[0]
    cap = pair_dev // steps
    orb_dev = held.shape[0]
    fit_rows = height - ENERGY_ROWS
    half = (pair_dev, width, width)
    energy = (pair_dev, 1, width)
    right = (steps, width // 2 + DIAGONAL_ROWS, width)
    return pl.pallas_call(
        functools.partial(pairs_kernel, cap, batch, parts, mask, right_mask),
        in_specs=[ANY()] * 5 + [VMEM()],
        out_specs=(ANY(), ANY(), ANY()),
        out_shape=(
            pltpu.HBM(half, jnp.bfloat16),
            pltpu.HBM(energy, jnp.float32),
            pltpu.HBM(right, jnp.bfloat16),
        ),
        scratch_shapes=[
            pltpu.SMEM(first.shape, jnp.int32),
            pltpu.SMEM(shift.shape, jnp.int32),
            pltpu.SMEM(occupied.shape, jnp.float32),
            pltpu.VMEM(rows.shape, jnp.float32),
            pltpu.VMEM((orb_dev + 1, fit_rows, width), jnp.bfloat16),
            pltpu.VMEM((steps, width, fit_rows), jnp.bfloat16),
            pltpu.VMEM(half, jnp.bfloat16),
            pltpu.VMEM(energy, jnp.float32),
            pltpu.VMEM(right, jnp.bfloat16),
            pltpu.SemaphoreType.DMA((4 + parts,)),
            pltpu.SemaphoreType.DMA((3, steps // batch)),
        ],
        compiler_params=pltpu.CompilerParams(vmem_limit_bytes=24 * MIB),
        name="pair_terms",
    )(*map(in_hbm, (first, shift, occupied, rows, held)), messages)


def left_kernel(batch, *refs):
    inputs, (density, pair_energy), scratch = refs[:5], refs[5:7], refs[7:]
    index, first, energy, halves, turns, inner, scattered, made, energies, arrived, left = scratch
    orb_dev, width, _ = inner.shape
    pair_dev = halves.shape[0]
    parts = pair_dev // batch

    def half(b):
        some = pl.ds(b * batch, batch)
        return pltpu.make_async_copy(inputs[3].at[some], halves.at[some], arrived.at[4 + b])

    def going(b):
        some = pl.ds(b * batch, batch)
        return pltpu.make_async_copy(made.at[some], density.at[some], left.at[b])

    loads = [
        pltpu.make_async_copy(inputs[n], target, arrived.at[n])
        for n, target in enumerate((index, first, energy))
    ]
    turns_load = pltpu.make_async_copy(inputs[4], turns, arrived.at[3])
    for load in loads:
        load.start()
    for b in range(parts):
        half(b).start()
    turns_load.start()
    inner[...] = jnp.zeros_like(inner)
    for load in loads:
        load.wait()

    def scatter(place, carry):
        scattered[index[place]] = energy[place]
        return carry

    lax.fori_loop(0, pair_dev, scatter, 0, unroll=8)
    gathered = scattered[...].reshape(pair_dev, width)
    energies[...] = -jnp.sum(gathered.T, axis=0, keepdims=True) / width
    energies_out = pltpu.make_async_copy(energies, pair_energy, left.at[orb_dev // batch])
    energies_out.start()

    def some_pairs(b, carry):
        half(b).wait()
        places = [b * batch + u for u in range(batch)]
        sums = [f32_dot(halves[place], halves[place], ((0,), (0,))) for place in places]
        for place, one in zip(places, sums):
            slot = first[place]
            inner[slot] = inner[slot] + one
        return carry

    lax.fori_loop(0, parts, some_pairs, 0)
    turns_load.wait()

    def some_slots(b, carry):
        slots = [b * batch + u for u in range(batch)]
        half_way = [turned(turns[slot], inner[slot]) for slot in slots]
        for slot, one in zip(slots, half_way):
            made[slot] = turned_back(one, turns[slot])
        going(b).start()
        return carry

    lax.fori_loop(0, orb_dev // batch, some_slots, 0)
    energies_out.wait()
    for b in range(orb_dev // batch):
        going(b).wait()


def left_density(index, first, energy, half, transforms, batch=8):
    orb_dev = transforms.shape[0]
    pair_dev, width, _ = half.shape
    density = (orb_dev, width, width)
    return pl.pallas_call(
        functools.partial(left_kernel, batch),
        in_specs=[ANY()] * 5,
        out_specs=(ANY(), ANY()),
        out_shape=(pltpu.HBM(density, jnp.float32), pltpu.HBM((1, pair_dev), jnp.float32)),
        scratch_shapes=[
            pltpu.SMEM(index.shape, jnp.int32),
            pltpu.SMEM(first.shape, jnp.int32),
            pltpu.VMEM(energy.shape, jnp.float32),
            pltpu.VMEM(half.shape, jnp.bfloat16),
            pltpu.VMEM(transforms.shape, jnp.bfloat16),
            pltpu.VMEM(density, jnp.float32),
            pltpu.VMEM(energy.shape, jnp.float32),
            pltpu.VMEM(density, jnp.float32),
            pltpu.VMEM((1, pair_dev), jnp.float32),
            pltpu.SemaphoreType.DMA((4 + pair_dev // batch,)),
            pltpu.SemaphoreType.DMA((orb_dev // batch + 1,)),
        ],
        compiler_params=pltpu.CompilerParams(vmem_limit_bytes=16 * MIB),
        name="left_density",
    )(*map(in_hbm, (index, first, energy, half, transforms)))


def right_kernel(
    batch, parts, asked_mask, mask, wanted, before, rights, transforms, out, asked, total, unfolded, turns, arrived, left
):
    senders = rights.shape[0]
    each = total.shape[0] // parts
    chunks = [pl.ds(c * each, each) for c in range(parts)]
    loads = [pltpu.make_async_copy(wanted, asked, arrived.at[0, parts])]
    for n, (source, target) in enumerate(((transforms, turns), (before, total))):
        for c, chunk in enumerate(chunks):
            loads.append(
                pltpu.make_async_copy(source.at[chunk], target.at[chunk], arrived.at[n, c])
            )
    for load in loads:
        load.start()

    def unfold(b, carry):
        for u in range(batch):
            full = unfold_symmetric(rights[b * batch + u].astype(jnp.float32))
            unfolded[b * batch + u] = full.astype(jnp.bfloat16)
        return carry

    lax.fori_loop(0, senders // batch, unfold, 0)
    for load in loads:
        load.wait()

    def some_messages(b, carry):
        places = [b * batch + u for u in range(batch)]
        slots = [asked[place ^ mask ^ asked_mask, 0, 0] for place in places]
        half_way = [
            f32_dot(turns[slot], unfolded[place], ((1,), (0,)))
            for slot, place in zip(slots, places)
        ]
        sums = [turned_back(one, turns[slot]) for slot, one in zip(slots, half_way)]
        for slot, one in zip(slots, sums):
            total[slot] = total[slot] + one
        return carry

    lax.fori_loop(0, senders // batch, some_messages, 0)

    stores = [
        pltpu.make_async_copy(total.at[chunk], out.at[chunk], left.at[c])
        for c, chunk in enumerate(chunks)
    ]
    for store in stores:
        store.start()
    for store in stores:
        store.wait()


def add_right_density(asked_mask, mask, asked, density, right, transforms, batch=16, parts=4):
    return pl.pallas_call(
        functools.partial(right_kernel, batch, parts, asked_mask, mask),
        in_specs=[ANY(), ANY(), VMEM(), ANY()],
        out_specs=ANY(),
        out_shape=pltpu.HBM(density.shape, jnp.float32),
        scratch_shapes=[
            pltpu.SMEM(asked.shape, jnp.int32),
            pltpu.VMEM(density.shape, jnp.float32),
            pltpu.VMEM((right.shape[0],) + density.shape[1:], jnp.bfloat16),
            pltpu.VMEM(transforms.shape, jnp.bfloat16),
            pltpu.SemaphoreType.DMA((2, parts + 1)),
            pltpu.SemaphoreType.DMA((parts,)),
        ],
        compiler_params=pltpu.CompilerParams(vmem_limit_bytes=16 * MIB),
        name="add_right_density",
    )(asked, in_hbm(density), right, in_hbm(transforms))


def exchange(messages, mask):
    groups = [[place ^ mask for place in range(messages.shape[0])]]
    return lax.all_to_all(
        messages, "orb", split_axis=0, concat_axis=0, tiled=True, axis_index_groups=groups
    )


def local(pair_list, orbital_slot, blocks, transforms, domain, eps_virt, eps_occ, offsets):
    owners = lax.axis_size("orb")
    orb_dev = blocks.shape[0]
    ask, send, give_back = owners // 2, owners // 2 + 1, 3 * owners // 4 + 1
    asked = exchange(wanted_slots(owners, orb_dev, ask, pair_list, orbital_slot), ask)
    rows, held = own_rotated(domain, eps_virt, blocks, transforms)
    incoming = exchange(pack_messages(ask, send, asked, held), send)
    index, first, shift, occupied = plan(
        owners, orb_dev, pair_list, orbital_slot, offsets, eps_occ
    )
    half, energy, right = pair_terms(
        send, give_back, first, shift, occupied, rows, held, incoming
    )
    came_back = exchange(right, give_back)
    density, pair_energy = left_density(index, first, energy, half, transforms)
    density = add_right_density(ask, give_back, asked, density, came_back, transforms)
    return (pair_energy.reshape(-1), density)


def solution(mesh):
    in_specs = (
        P(("groups", "orb"), None),
        P("groups"),
        P(("groups", "orb"), None, None),
        P(("groups", "orb"), None, None),
        P(("groups", "orb"), None),
        P("groups"),
        P("groups"),
        P("groups"),
    )
    out_specs = (P(("groups", "orb")), P(("groups", "orb"), None, None))
    return jax.shard_map(local, mesh=mesh, in_specs=in_specs, out_specs=out_specs, check_vma=False)
```

```python
import functools

import jax
import jax.numpy as jnp
from jax import lax
from jax.experimental import pallas as pl
from jax.experimental.pallas import tpu as pltpu
from jax.sharding import PartitionSpec as P

AUXBLK = 128
ENERGY_ROWS = 16
DIAGONAL_ROWS = 16
MIB = 1024 * 1024

SMEM = functools.partial(pl.BlockSpec, memory_space=pltpu.SMEM)
VMEM = functools.partial(pl.BlockSpec, memory_space=pltpu.VMEM)
ANY = functools.partial(pl.BlockSpec, memory_space=pl.ANY)


def in_hbm(array):
    return pltpu.with_memory_space_constraint(array, pltpu.HBM)


def f32_dot(lhs, rhs, dims):
    return lax.dot_general(lhs, rhs, (dims, ((), ())), preferred_element_type=jnp.float32)


def in_two_parts(value):
    high = value.astype(jnp.bfloat16)
    return high, (value - high.astype(jnp.float32)).astype(jnp.bfloat16)


def turned(turn, inner):
    width = inner.shape[1]
    both = f32_dot(turn, jnp.concatenate(in_two_parts(inner), axis=1), ((1,), (0,)))
    return both[:, :width] + both[:, width:]


def turned_back(half_way, turn):
    height = half_way.shape[0]
    both = f32_dot(jnp.concatenate(in_two_parts(half_way), axis=0), turn, ((1,), (1,)))
    return both[:height] + both[height:]


def wanted_kernel(orb_dev, mask, pairs, slots, wanted):
    def one_pair(pair, carry):
        slot = slots[pairs[1, pair]]
        owner = lax.div(slot, jnp.int32(orb_dev))
        local_slot = lax.rem(slot, jnp.int32(orb_dev))
        wanted[owner ^ mask] = jnp.full(wanted.shape[1:], local_slot, jnp.int32)
        return carry

    lax.fori_loop(0, pairs.shape[1], one_pair, 0, unroll=16)


def wanted_slots(owners, orb_dev, mask, pair_list, orbital_slot):
    return pl.pallas_call(
        functools.partial(wanted_kernel, orb_dev, mask),
        out_shape=pltpu.HBM((owners, 1, 128), jnp.int32),
        in_specs=[SMEM()] * 2,
        out_specs=VMEM(),
        name="wanted_slots",
    )(*map(in_hbm, (pair_list.T, orbital_slot)))


def plan_kernel(orb_dev, cap, pairs, slots, offsets, eps_occ, index, first, shift, occupied, seen):
    owners = seen.shape[0]

    def clear(owner, carry):
        seen[owner] = 0
        return carry

    lax.fori_loop(0, owners, clear, 0, unroll=8)

    def one_pair(pair, carry):
        slot_i = slots[pairs[0, pair]]
        slot_j = slots[pairs[1, pair]]
        owner = lax.div(slot_j, jnp.int32(orb_dev))
        rank = seen[owner]
        seen[owner] = rank + 1
        place = owner * cap + rank
        index[place] = pair
        first[place] = lax.rem(slot_i, jnp.int32(orb_dev))
        shift[place] = offsets[slot_i] - offsets[slot_j]
        occupied[place] = eps_occ[slot_i] + eps_occ[slot_j]
        return carry

    lax.fori_loop(0, pairs.shape[1], one_pair, 0, unroll=8)


def plan(owners, orb_dev, pair_list, orbital_slot, offsets, eps_occ):
    pair_dev = pair_list.shape[0]
    cap = pair_dev // owners
    sorted_ints = pltpu.HBM((pair_dev,), jnp.int32)
    return pl.pallas_call(
        functools.partial(plan_kernel, orb_dev, cap),
        out_shape=(
            sorted_ints,
            sorted_ints,
            sorted_ints,
            pltpu.HBM((pair_dev,), jnp.float32),
        ),
        in_specs=[SMEM()] * 4,
        out_specs=(SMEM(), SMEM(), SMEM(), SMEM()),
        scratch_shapes=[pltpu.SMEM((owners,), jnp.int32)],
        name="plan",
    )(*map(in_hbm, (pair_list.T, orbital_slot, offsets, eps_occ)))


def own_kernel(
    chunk, domain, eps_virt, blocks, transforms, rows, held, wanted, table, found, block_rows, turns, made, arrived, left
):
    orb_dev, fit_rows, width = blocks.shape
    chunks = orb_dev // chunk

    def coming(c):
        part = pl.ds(c * chunk, chunk)
        return (
            pltpu.make_async_copy(blocks.at[part], block_rows.at[part], arrived.at[0, c]),
            pltpu.make_async_copy(transforms.at[part], turns.at[part], arrived.at[1, c]),
        )

    def going(c):
        part = pl.ds(c * chunk, chunk)
        return pltpu.make_async_copy(made.at[part], held.at[part], left.at[c])

    loads = [
        pltpu.make_async_copy(domain, wanted, arrived.at[0, chunks]),
        pltpu.make_async_copy(eps_virt, table, arrived.at[1, chunks]),
    ]
    for load in loads:
        load.start()
    for c in range(chunks):
        for copy in coming(c):
            copy.start()
    for load in loads:
        load.wait()
    line, lane = wanted[...] // 128, wanted[...] % 128
    energies = jnp.zeros((orb_dev, width), jnp.float32)
    for k in range(table.shape[0]):
        spread = jnp.broadcast_to(table[pl.ds(k, 1), :], (orb_dev, width))
        picked = jnp.take_along_axis(spread, lane, axis=1)
        energies = jnp.where(line == k, picked, energies)
    rounded = energies.astype(jnp.bfloat16).astype(jnp.float32)
    for s in range(orb_dev):
        row = rounded[s : s + 1, :]
        found[s] = row
        made[s, fit_rows:, :] = jnp.broadcast_to(row, (ENERGY_ROWS, width)).astype(jnp.bfloat16)
    rows_out = pltpu.make_async_copy(found, rows, left.at[chunks])
    rows_out.start()

    def one_chunk(c, carry):
        for copy in coming(c):
            copy.wait()
        slots = [c * chunk + u for u in range(chunk)]
        rotated = [f32_dot(block_rows[slot], turns[slot], ((1,), (0,))) for slot in slots]
        for slot, one in zip(slots, rotated):
            made[slot, :fit_rows, :] = one.astype(jnp.bfloat16)
        going(c).start()
        return carry

    lax.fori_loop(0, chunks, one_chunk, 0)
    rows_out.wait()
    for c in range(chunks):
        going(c).wait()


def own_rotated(domain, eps_virt, blocks, transforms, chunk=8):
    orb_dev, fit_rows, width = blocks.shape
    shape = (orb_dev, fit_rows + ENERGY_ROWS, width)
    table = (eps_virt.shape[0] // 128, 128)
    return pl.pallas_call(
        functools.partial(own_kernel, chunk),
        in_specs=[ANY()] * 4,
        out_specs=(ANY(), ANY()),
        out_shape=(
            pltpu.HBM((orb_dev, 1, width), jnp.float32),
            pltpu.HBM(shape, jnp.bfloat16),
        ),
        scratch_shapes=[
            pltpu.VMEM(domain.shape, jnp.int32),
            pltpu.VMEM(table, jnp.float32),
            pltpu.VMEM((orb_dev, 1, width), jnp.float32),
            pltpu.VMEM(blocks.shape, jnp.bfloat16),
            pltpu.VMEM(transforms.shape, jnp.bfloat16),
            pltpu.VMEM(shape, jnp.bfloat16),
            pltpu.SemaphoreType.DMA((2, orb_dev // chunk + 1)),
            pltpu.SemaphoreType.DMA((orb_dev // chunk + 1,)),
        ],
        compiler_params=pltpu.CompilerParams(vmem_limit_bytes=16 * MIB),
        name="own_rotated",
    )(*map(in_hbm, (domain, eps_virt.reshape(table), blocks, transforms)))


def pack_kernel(asked_mask, mask, asked, held, messages, made, arrived, left):
    owners = messages.shape[0]

    def coming(owner):
        source = held.at[asked[owner ^ asked_mask, 0, 0]]
        return pltpu.make_async_copy(source, made.at[owner], arrived.at[owner])

    def going(owner):
        return pltpu.make_async_copy(made.at[owner], messages.at[owner ^ mask], left.at[owner])

    def start(owner, carry):
        coming(owner).start()
        return carry

    def forward(owner, carry):
        coming(owner).wait()
        going(owner).start()
        return carry

    def finish(owner, carry):
        going(owner).wait()
        return carry

    for step in (start, forward, finish):
        lax.fori_loop(0, owners, step, 0, unroll=4)


def pack_messages(asked_mask, mask, asked, held):
    owners = asked.shape[0]
    shape = (owners,) + held.shape[1:]
    return pl.pallas_call(
        functools.partial(pack_kernel, asked_mask, mask),
        in_specs=[SMEM(), ANY()],
        out_specs=ANY(),
        out_shape=pltpu.HBM(shape, jnp.bfloat16),
        scratch_shapes=[
            pltpu.VMEM(shape, jnp.bfloat16),
            pltpu.SemaphoreType.DMA((owners,)),
            pltpu.SemaphoreType.DMA((owners,)),
        ],
        compiler_params=pltpu.CompilerParams(vmem_limit_bytes=16 * MIB),
        name="pack_messages",
    )(asked, in_hbm(held))


def fold_symmetric(full):
    width = full.shape[0]
    mid = width // 2
    row = lax.broadcasted_iota(jnp.int32, (mid, width), 0)
    lane = lax.broadcasted_iota(jnp.int32, (mid, width), 1)
    upper, lower = full[:mid, :], full[mid:, :]
    folded = jnp.where(lane <= row + mid, pltpu.roll(upper, mid, 1), lower)
    diagonal = jnp.sum(jnp.where(lane == row + mid, lower, 0.0), axis=0, keepdims=True)
    return jnp.concatenate([folded, jnp.broadcast_to(diagonal, (DIAGONAL_ROWS, width))], axis=0)


def unfold_symmetric(folded):
    width = folded.shape[1]
    mid = width // 2
    row = lax.broadcasted_iota(jnp.int32, (mid, width), 0)
    lane = lax.broadcasted_iota(jnp.int32, (mid, width), 1)
    body, diagonal = folded[:mid, :], folded[mid : mid + 1, :]
    moved = pltpu.roll(body, mid, 1)
    upper = jnp.where(lane < row, moved, 0.0) + jnp.where(lane >= mid, moved, 0.0)
    upper = upper + jnp.where(lane == row, 0.5 * moved, 0.0)
    lower = jnp.where(lane > row + mid, body, 0.0)
    lower = lower + jnp.where(lane == row + mid, 0.5 * diagonal, 0.0)
    once = jnp.concatenate([upper, lower], axis=0)
    return once + once.T


def pairs_kernel(cap, batch, parts, mask, right_mask, *refs):
    inputs, (half, energy, right), scratch = refs[:5], refs[6:9], refs[9:]
    came = refs[5]
    first, shift, occupied, rows, held, turned_over, halves, energies, rights, arrived, left = scratch
    steps, height, width = came.shape
    fit_rows = height - ENERGY_ROWS
    block_count = fit_rows // AUXBLK
    orb_dev = rows.shape[0]
    each = orb_dev // parts

    def own(c):
        slots = pl.ds(c * each, each)
        source = inputs[4].at[slots, pl.ds(0, fit_rows)]
        return pltpu.make_async_copy(source, held.at[slots], arrived.at[4 + c])

    loads = [
        pltpu.make_async_copy(source, target, arrived.at[n])
        for n, (source, target) in enumerate(zip(inputs[:4], (first, shift, occupied, rows)))
    ] + [own(c) for c in range(parts)]
    for load in loads:
        load.start()

    def going(b):
        some = pl.ds(b * batch * cap, batch * cap)
        few = pl.ds((b * batch) ^ (right_mask // batch * batch), batch)
        return (
            pltpu.make_async_copy(halves.at[some], half.at[some], left.at[0, b]),
            pltpu.make_async_copy(energies.at[some], energy.at[some], left.at[1, b]),
            pltpu.make_async_copy(rights.at[few], right.at[few], left.at[2, b]),
        )

    held[orb_dev, :AUXBLK, :] = jnp.zeros((AUXBLK, width), jnp.bfloat16)

    def turn_over(b, carry):
        for u in range(batch):
            turned_over[b * batch + u] = came[b * batch + u, :fit_rows, :].T
        return carry

    lax.fori_loop(0, steps // batch, turn_over, 0)
    for load in loads:
        load.wait()

    def shifted(place):
        moved = []
        for block in range(block_count):
            source = block - shift[place]
            inside = (source >= 0) & (source < block_count)
            slot = jnp.where(inside, first[place], orb_dev)
            begin = pl.multiple_of(jnp.where(inside, source, 0) * AUXBLK, AUXBLK)
            moved.append(held[slot, pl.ds(begin, AUXBLK), :])
        return jnp.concatenate(moved, axis=0)

    def one_batch(b, carry):
        group = [b * batch + u for u in range(batch)]
        couplings, far = [], []
        for step in group:
            side = jnp.concatenate([shifted(step * cap + k) for k in range(cap)], axis=1)
            couplings.append(f32_dot(turned_over[step ^ mask], side, ((1,), (0,))))
            row = came[step ^ mask, fit_rows:, :].astype(jnp.float32)[:1, :]
            far.append(jnp.broadcast_to(row, (width, width)).T)
        for u, step in enumerate(group):
            sides = []
            for k in range(cap):
                place = step * cap + k
                coupling = couplings[u][:, k * width : (k + 1) * width]
                amplitude = coupling / (far[u] + (rows[first[place]] - occupied[place]))
                energies[place] = jnp.sum(coupling * amplitude, axis=0, keepdims=True)
                sides.append(amplitude.astype(jnp.bfloat16))
                halves[place] = sides[-1]
            side = jnp.concatenate(sides, axis=1)
            density = f32_dot(side, side, ((1,), (1,)))
            rights[step ^ right_mask] = fold_symmetric(density).astype(jnp.bfloat16)
        for copy in going(b):
            copy.start()
        return carry

    def finish(b, carry):
        for copy in going(b):
            copy.wait()
        return carry

    lax.fori_loop(0, steps // batch, one_batch, 0)
    lax.fori_loop(0, steps // batch, finish, 0)


def pair_terms(
    mask, right_mask, first, shift, occupied, rows, held, messages, batch=8, parts=8
):
    steps, height, width = messages.shape
    pair_dev = first.shape[0]
    cap = pair_dev // steps
    orb_dev = held.shape[0]
    fit_rows = height - ENERGY_ROWS
    half = (pair_dev, width, width)
    energy = (pair_dev, 1, width)
    right = (steps, width // 2 + DIAGONAL_ROWS, width)
    return pl.pallas_call(
        functools.partial(pairs_kernel, cap, batch, parts, mask, right_mask),
        in_specs=[ANY()] * 5 + [VMEM()],
        out_specs=(ANY(), ANY(), ANY()),
        out_shape=(
            pltpu.HBM(half, jnp.bfloat16),
            pltpu.HBM(energy, jnp.float32),
            pltpu.HBM(right, jnp.bfloat16),
        ),
        scratch_shapes=[
            pltpu.SMEM(first.shape, jnp.int32),
            pltpu.SMEM(shift.shape, jnp.int32),
            pltpu.SMEM(occupied.shape, jnp.float32),
            pltpu.VMEM(rows.shape, jnp.float32),
            pltpu.VMEM((orb_dev + 1, fit_rows, width), jnp.bfloat16),
            pltpu.VMEM((steps, width, fit_rows), jnp.bfloat16),
            pltpu.VMEM(half, jnp.bfloat16),
            pltpu.VMEM(energy, jnp.float32),
            pltpu.VMEM(right, jnp.bfloat16),
            pltpu.SemaphoreType.DMA((4 + parts,)),
            pltpu.SemaphoreType.DMA((3, steps // batch)),
        ],
        compiler_params=pltpu.CompilerParams(vmem_limit_bytes=24 * MIB),
        name="pair_terms",
    )(*map(in_hbm, (first, shift, occupied, rows, held)), messages)


def left_kernel(batch, *refs):
    inputs, (density, pair_energy), scratch = refs[:5], refs[5:7], refs[7:]
    index, first, energy, halves, turns, inner, scattered, made, energies, arrived, left = scratch
    orb_dev, width, _ = inner.shape
    pair_dev = halves.shape[0]
    parts = pair_dev // batch

    def half(b):
        some = pl.ds(b * batch, batch)
        return pltpu.make_async_copy(inputs[3].at[some], halves.at[some], arrived.at[4 + b])

    def going(b):
        some = pl.ds(b * batch, batch)
        return pltpu.make_async_copy(made.at[some], density.at[some], left.at[b])

    loads = [
        pltpu.make_async_copy(inputs[n], target, arrived.at[n])
        for n, target in enumerate((index, first, energy))
    ]
    turns_load = pltpu.make_async_copy(inputs[4], turns, arrived.at[3])
    for load in loads:
        load.start()
    for b in range(parts):
        half(b).start()
    turns_load.start()
    inner[...] = jnp.zeros_like(inner)
    for load in loads:
        load.wait()

    def scatter(place, carry):
        scattered[index[place]] = energy[place]
        return carry

    lax.fori_loop(0, pair_dev, scatter, 0, unroll=8)
    gathered = scattered[...].reshape(pair_dev, width)
    energies[...] = -jnp.sum(gathered.T, axis=0, keepdims=True) / width
    energies_out = pltpu.make_async_copy(energies, pair_energy, left.at[orb_dev // batch])
    energies_out.start()

    def some_pairs(b, carry):
        half(b).wait()
        places = [b * batch + u for u in range(batch)]
        sums = [f32_dot(halves[place], halves[place], ((0,), (0,))) for place in places]
        for place, one in zip(places, sums):
            slot = first[place]
            inner[slot] = inner[slot] + one
        return carry

    lax.fori_loop(0, parts, some_pairs, 0)
    turns_load.wait()

    def some_slots(b, carry):
        slots = [b * batch + u for u in range(batch)]
        half_way = [turned(turns[slot], inner[slot]) for slot in slots]
        for slot, one in zip(slots, half_way):
            made[slot] = turned_back(one, turns[slot])
        going(b).start()
        return carry

    lax.fori_loop(0, orb_dev // batch, some_slots, 0)
    energies_out.wait()
    for b in range(orb_dev // batch):
        going(b).wait()


def left_density(index, first, energy, half, transforms, batch=8):
    orb_dev = transforms.shape[0]
    pair_dev, width, _ = half.shape
    density = (orb_dev, width, width)
    return pl.pallas_call(
        functools.partial(left_kernel, batch),
        in_specs=[ANY()] * 5,
        out_specs=(ANY(), ANY()),
        out_shape=(pltpu.HBM(density, jnp.float32), pltpu.HBM((1, pair_dev), jnp.float32)),
        scratch_shapes=[
            pltpu.SMEM(index.shape, jnp.int32),
            pltpu.SMEM(first.shape, jnp.int32),
            pltpu.VMEM(energy.shape, jnp.float32),
            pltpu.VMEM(half.shape, jnp.bfloat16),
            pltpu.VMEM(transforms.shape, jnp.bfloat16),
            pltpu.VMEM(density, jnp.float32),
            pltpu.VMEM(energy.shape, jnp.float32),
            pltpu.VMEM(density, jnp.float32),
            pltpu.VMEM((1, pair_dev), jnp.float32),
            pltpu.SemaphoreType.DMA((4 + pair_dev // batch,)),
            pltpu.SemaphoreType.DMA((orb_dev // batch + 1,)),
        ],
        compiler_params=pltpu.CompilerParams(vmem_limit_bytes=16 * MIB),
        name="left_density",
    )(*map(in_hbm, (index, first, energy, half, transforms)))


def right_kernel(
    batch, parts, asked_mask, mask, wanted, before, rights, transforms, out, asked, total, unfolded, turns, arrived, left
):
    senders = rights.shape[0]
    each = total.shape[0] // parts
    chunks = [pl.ds(c * each, each) for c in range(parts)]
    loads = [pltpu.make_async_copy(wanted, asked, arrived.at[0, parts])]
    for n, (source, target) in enumerate(((transforms, turns), (before, total))):
        for c, chunk in enumerate(chunks):
            loads.append(
                pltpu.make_async_copy(source.at[chunk], target.at[chunk], arrived.at[n, c])
            )
    for load in loads:
        load.start()

    def unfold(b, carry):
        for u in range(batch):
            full = unfold_symmetric(rights[b * batch + u].astype(jnp.float32))
            unfolded[b * batch + u] = full.astype(jnp.bfloat16)
        return carry

    lax.fori_loop(0, senders // batch, unfold, 0)
    for load in loads:
        load.wait()

    def some_messages(b, carry):
        places = [b * batch + u for u in range(batch)]
        slots = [asked[place ^ mask ^ asked_mask, 0, 0] for place in places]
        half_way = [
            f32_dot(turns[slot], unfolded[place], ((1,), (0,)))
            for slot, place in zip(slots, places)
        ]
        sums = [turned_back(one, turns[slot]) for slot, one in zip(slots, half_way)]
        for slot, one in zip(slots, sums):
            total[slot] = total[slot] + one
        return carry

    lax.fori_loop(0, senders // batch, some_messages, 0)

    stores = [
        pltpu.make_async_copy(total.at[chunk], out.at[chunk], left.at[c])
        for c, chunk in enumerate(chunks)
    ]
    for store in stores:
        store.start()
    for store in stores:
        store.wait()


def add_right_density(asked_mask, mask, asked, density, right, transforms, batch=16, parts=4):
    return pl.pallas_call(
        functools.partial(right_kernel, batch, parts, asked_mask, mask),
        in_specs=[ANY(), ANY(), VMEM(), ANY()],
        out_specs=ANY(),
        out_shape=pltpu.HBM(density.shape, jnp.float32),
        scratch_shapes=[
            pltpu.SMEM(asked.shape, jnp.int32),
            pltpu.VMEM(density.shape, jnp.float32),
            pltpu.VMEM((right.shape[0],) + density.shape[1:], jnp.bfloat16),
            pltpu.VMEM(transforms.shape, jnp.bfloat16),
            pltpu.SemaphoreType.DMA((2, parts + 1)),
            pltpu.SemaphoreType.DMA((parts,)),
        ],
        compiler_params=pltpu.CompilerParams(vmem_limit_bytes=16 * MIB),
        name="add_right_density",
    )(asked, in_hbm(density), right, in_hbm(transforms))


def exchange(messages, mask):
    groups = [[place ^ mask for place in range(messages.shape[0])]]
    return lax.all_to_all(
        messages, "orb", split_axis=0, concat_axis=0, tiled=True, axis_index_groups=groups
    )


def local(pair_list, orbital_slot, blocks, transforms, domain, eps_virt, eps_occ, offsets):
    owners = lax.axis_size("orb")
    orb_dev = blocks.shape[0]
    ask, send, give_back = owners // 2, owners // 2 + 1, 3 * owners // 4 + 1
    asked = exchange(wanted_slots(owners, orb_dev, ask, pair_list, orbital_slot), ask)
    rows, held = own_rotated(domain, eps_virt, blocks, transforms)
    incoming = exchange(pack_messages(ask, send, asked, held), send)
    index, first, shift, occupied = plan(
        owners, orb_dev, pair_list, orbital_slot, offsets, eps_occ
    )
    half, energy, right = pair_terms(
        send, give_back, first, shift, occupied, rows, held, incoming
    )
    came_back = exchange(right, give_back)
    density, pair_energy = left_density(index, first, energy, half, transforms)
    density = add_right_density(ask, give_back, asked, density, came_back, transforms)
    return (pair_energy.reshape(-1), density)


def solution(mesh):
    in_specs = (
        P(("groups", "orb"), None),
        P("groups"),
        P(("groups", "orb"), None, None),
        P(("groups", "orb"), None, None),
        P(("groups", "orb"), None),
        P("groups"),
        P("groups"),
        P("groups"),
    )
    out_specs = (P(("groups", "orb")), P(("groups", "orb"), None, None))
    return jax.shard_map(local, mesh=mesh, in_specs=in_specs, out_specs=out_specs, check_vma=False)
```
